32 devices in a mesh: chan: 8 (over y, x, core), bl: 4 (over z).
Axes of the slice: x: 2, y: 2, z: 4, core: 2. Of those that a mesh axis runs over, the one named last changes fastest.
Arguments:
- visibilities: float32 [2, 2, 192, 8192], P(None, None, 'chan', 'bl'), may hold values from -12 to 12
- coherencies: bfloat16 [2, 4, 2, 192, 8192], P(None, None, None, 'chan', 'bl'), may hold values from -6 to 6
- start_gains: float32 [2, 4, 2, 192, 512], P(None, None, None, 'chan'), may hold values from -4 to 4
- penalty: float32 [4], replicated, may hold values from 100 to 1000
- stations: int32 [2, 8192], P(None, 'bl'), may hold values from 0 to 511, as said below
Outputs:
- gains: float32 [2, 4, 2, 192, 512], P(None, None, None, 'chan')
- consensus: float32 [2, 4, 2, 192, 512], P(None, None, None, 'chan', 'bl')
- dual: float32 [2, 4, 2, 192, 512], P(None, None, None, 'chan', 'bl')
The draws below stay inside these ranges and needn't reach their ends.
Inputs may be any that keep to these rules, and one draw needn't show every extreme that they name: Each baseline joins two different stations.
All inputs are finite; a program needn't handle non-finite values.
Results may differ from the reference program's by a relative error of at most 0.0003.
Values sent between devices are 32-bit elements; how exact they have to be, the bound alone decides.
No kernel may reach another device: no remote copies, remote signals or barrier semaphores. Data moves between devices by JAX's collectives and lax.ppermute only.
A program may use at most 64 MiB of HBM per device.

```python
import math
import jax
import jax.numpy as jnp
from jax import lax

S = 512
K = 4
TIMES = 2
POLY = 4
ITERS = 2
F = 192
B = 8192


def draw_stations(key, part):
    key = jax.random.fold_in(key, 7)
    first_key, offset_key = jax.random.split(key)
    first = jax.random.randint(first_key, (B,), 0, S)
    offset = jax.random.randint(offset_key, (B,), 1, S)
    second = (first + offset) % S
    return jnp.stack([first, second]).astype(jnp.int32)


def steps_of(own_key, dims, cuts, least, high):
    gain, own = 1.0, jax.random.fold_in(own_key, 6)
    for dim, shards_of in cuts:
        heights = jnp.exp(jax.random.uniform(jax.random.fold_in(own, dim), (shards_of,), jnp.float32, least / len(cuts), high / len(cuts)))
        gain = gain * jnp.repeat(heights, dims[dim] // shards_of).reshape([-1 if axis == dim else 1 for axis in range(len(dims))])
    return gain


def bell_draw(key, extent, spread, reach, cuts=(), kind=jnp.bfloat16):
    entries = spread * jax.random.normal(key, extent, jnp.float32)
    if cuts:
        entries = entries * steps_of(key, extent, cuts, -0.22, 0.18)
    return jnp.clip(entries, -reach, reach).astype(kind)


def setup_inputs(seed: int = 0) -> dict:
    streams_of = jax.random.split(jax.random.key(seed), 6)
    visibilities = bell_draw(streams_of[0], (2, TIMES, F, B), 2.0, 12.0, ((2, 8), (3, 4)), jnp.float32)
    coherencies = bell_draw(streams_of[1], (2, K, TIMES, F, B), 1.0, 6.0, ((3, 8), (4, 4)))
    start_gains = bell_draw(streams_of[2], (2, K, TIMES, F, S), 0.7, 4.0, ((3, 8),), jnp.float32)
    penalty = jnp.clip(jnp.exp(jax.random.uniform(streams_of[3], (K,), jnp.float32, math.log(100.0), math.log(1000.0))), 100.0, 1000.0)
    stations = draw_stations(jax.random.fold_in(streams_of[5], 71), 0)
    return {"visibilities": visibilities, "coherencies": coherencies, "start_gains": start_gains, "penalty": penalty, "stations": stations}


def bernstein(rows, total):
    position = (rows.astype(jnp.float32) + 0.5) / total
    columns = [math.comb(POLY - 1, degree) * position ** degree * (1.0 - position) ** (POLY - 1 - degree) for degree in range(POLY)]
    return jnp.stack(columns, axis=1)

def normals(visibility, coherency, gains, first, second):
    coh_real = coherency[0].astype(jnp.float32)
    coh_imag = coherency[1].astype(jnp.float32)
    first_real = jnp.take(gains[0], first, axis=3)
    first_imag = jnp.take(gains[1], first, axis=3)
    second_real = jnp.take(gains[0], second, axis=3)
    second_imag = jnp.take(gains[1], second, axis=3)
    pair_real = first_real * second_real + first_imag * second_imag
    pair_imag = first_imag * second_real - first_real * second_imag
    model_real = pair_real * coh_real - pair_imag * coh_imag
    model_imag = pair_real * coh_imag + pair_imag * coh_real
    resid_real = visibility[0] - jnp.sum(model_real, axis=0) + model_real
    resid_imag = visibility[1] - jnp.sum(model_imag, axis=0) + model_imag
    power = coh_real * coh_real + coh_imag * coh_imag
    left_real = second_real * coh_real + second_imag * coh_imag
    left_imag = second_imag * coh_real - second_real * coh_imag
    right_real = first_real * coh_real - first_imag * coh_imag
    right_imag = first_real * coh_imag + first_imag * coh_real
    first_terms = jnp.stack([resid_real * left_real - resid_imag * left_imag, resid_real * left_imag + resid_imag * left_real, (second_real * second_real + second_imag * second_imag) * power])
    second_terms = jnp.stack([resid_real * right_real + resid_imag * right_imag, resid_real * right_imag - resid_imag * right_real, (first_real * first_real + first_imag * first_imag) * power])
    terms = jnp.concatenate([first_terms, second_terms], axis=4)
    station_index = jnp.concatenate([first, second]).astype(jnp.int32)
    shape = terms.shape[:4] + (gains.shape[4],)
    return jnp.zeros(shape, jnp.float32).at[:, :, :, :, station_index].add(terms)

def update(normal, target, penalty):
    weight = penalty[:, None, None, None]
    divisor = normal[2] + weight
    return jnp.stack([(normal[0] + weight * target[0]) / divisor, (normal[1] + weight * target[1]) / divisor])

def reference(visibilities, coherencies, start_gains, penalty, stations):
    first = stations[0]
    second = stations[1]
    highest = lax.Precision.HIGHEST

    def per_channel(items):
        vis_one, coh_one, gain_one = items
        result = normals(vis_one[:, :, None], coh_one[:, :, :, None], gain_one[:, :, :, None], first, second)
        return result[:, :, :, 0]
    bern_rows = bernstein(jnp.arange(F, dtype=jnp.int32), F)
    gram_matrix = jnp.dot(bern_rows.T, bern_rows, precision=highest)
    factor = jnp.linalg.cholesky(gram_matrix)
    gains = start_gains
    consensus = start_gains
    dual = jnp.zeros_like(start_gains)
    for iteration in range(ITERS):
        stacked = lax.map(per_channel, (jnp.moveaxis(visibilities, 2, 0), jnp.moveaxis(coherencies, 3, 0), jnp.moveaxis(gains, 3, 0)))
        normal = jnp.moveaxis(stacked, 0, 3)
        gains = update(normal, consensus - dual, penalty)
        partial_value = jnp.einsum('fj,rktfs->jrkts', bern_rows, gains + dual, precision=highest)
        coefficients = jax.scipy.linalg.cho_solve((factor, True), partial_value.reshape(POLY, -1)).reshape(partial_value.shape)
        consensus = jnp.einsum('fj,jrkts->rktfs', bern_rows, coefficients, precision=highest)
        dual = dual + gains - consensus
    return (gains, consensus, dual)
```

```python
import functools
import math

import jax
import jax.numpy as jnp
import numpy as np
from jax import lax
from jax.experimental import pallas as pl
from jax.experimental.pallas import tpu as pltpu
from jax.sharding import PartitionSpec as P

POLY = 4
ITERS = 2
ROWS_BY_COLS = (((1,), (0,)), ((), ()))
ROWS_BY_ROWS = (((1,), (1,)), ((), ()))


def bernstein_tables(total):
    position = (np.arange(total) + 0.5) / total
    basis = np.stack(
        [math.comb(POLY - 1, j) * position**j * (1.0 - position) ** (POLY - 1 - j) for j in range(POLY)], axis=1
    )
    factor = np.linalg.cholesky(basis.T @ basis)
    solved = np.linalg.solve(factor.T, np.linalg.solve(factor, basis.T)).T
    return basis.astype(np.float32), solved.astype(np.float32)


def split(values):
    upper = values.astype(jnp.bfloat16)
    return upper, (values - upper.astype(jnp.float32)).astype(jnp.bfloat16)


def normals_kernel(dirs, chans, *refs):
    gain_refs = refs[:2]
    vis_ref, coh_ref, station_ref = refs[2:5]
    out_refs = refs[5:7]
    parts = refs[7]
    step = pl.program_id(0)
    half = dirs // 2
    count = gain_refs[0].shape[-1]
    rows = 2 * dirs * chans
    width = station_ref.shape[1]

    @pl.when(step == 0)
    def _():
        pieces = [ref[part] for part in range(2) for ref in gain_refs]
        upper, lower = split(jnp.concatenate(pieces, axis=0).reshape(rows, count))
        parts[0] = upper
        parts[1] = lower

    ids = lax.broadcasted_iota(jnp.int32, (count, width), 0)
    picks = [(ids == station_ref[end : end + 1, :]).astype(jnp.float32).astype(jnp.bfloat16) for end in range(2)]
    dot = functools.partial(lax.dot_general, preferred_element_type=jnp.float32)
    first, second = [
        dot(parts[0], pick, ROWS_BY_COLS) + dot(parts[1], pick, ROWS_BY_COLS) for pick in picks
    ]

    def row(values, part, k):
        start = (part * dirs + k) * chans
        return values[start : start + chans]

    rest_real = vis_ref[0, 0]
    rest_imag = vis_ref[1, 0]
    sides = []
    for k in range(dirs):
        coh_real = coh_ref[0, k, 0].astype(jnp.float32)
        coh_imag = coh_ref[1, k, 0].astype(jnp.float32)
        first_real, first_imag = row(first, 0, k), row(first, 1, k)
        second_real, second_imag = row(second, 0, k), row(second, 1, k)
        left_real = second_real * coh_real + second_imag * coh_imag
        left_imag = second_imag * coh_real - second_real * coh_imag
        right_real = first_real * coh_real - first_imag * coh_imag
        right_imag = first_real * coh_imag + first_imag * coh_real
        rest_real = rest_real - (first_real * left_real + first_imag * left_imag)
        rest_imag = rest_imag - (first_imag * left_real - first_real * left_imag)
        sides.append((left_real, left_imag, right_real, right_imag))
    first_terms = []
    second_terms = []
    for group in range(2):
        chosen = sides[group * half : (group + 1) * half]
        first_terms += [rest_real * a - rest_imag * b for a, b, _, _ in chosen]
        first_terms += [rest_real * b + rest_imag * a for a, b, _, _ in chosen]
        first_terms += [a * a + b * b for a, b, _, _ in chosen]
        second_terms += [rest_real * c + rest_imag * d for _, _, c, d in chosen]
        second_terms += [rest_real * d - rest_imag * c for _, _, c, d in chosen]
        second_terms += [c * c + d * d for _, _, c, d in chosen]
    total = None
    for pick, terms in zip(picks, (first_terms, second_terms)):
        for piece in split(jnp.concatenate(terms, axis=0)):
            value = dot(piece, pick, ROWS_BY_ROWS)
            total = value if total is None else total + value
    total = total.reshape(2, 3, half, chans, count)
    for group in range(2):
        ref = out_refs[group]

        @pl.when(step == 0)
        def _():
            ref[...] = total[group]

        @pl.when(step > 0)
        def _():
            ref[...] += total[group]


def normals(gains, visibilities, coherencies, stations, time):
    _, half, chans, count = gains[0].shape
    dirs = 2 * half
    links = visibilities.shape[3]
    width = min(1024, links)
    gain_spec = pl.BlockSpec((2, half, chans, count), lambda i: (0, 0, 0, 0))
    out_spec = pl.BlockSpec((3, half, chans, count), lambda i: (0, 0, 0, 0))
    flops = 2 * 2 * links * count * (2 * 2 * dirs * chans + 2 * 3 * dirs * chans)
    return pl.pallas_call(
        functools.partial(normals_kernel, dirs, chans),
        grid=(links // width,),
        in_specs=[
            gain_spec,
            gain_spec,
            pl.BlockSpec((2, 1, chans, width), lambda i: (0, time, 0, i)),
            pl.BlockSpec((2, dirs, 1, chans, width), lambda i: (0, 0, time, 0, i)),
            pl.BlockSpec((2, width), lambda i: (0, i)),
        ],
        out_specs=[out_spec, out_spec],
        out_shape=[jax.ShapeDtypeStruct((3, half, chans, count), jnp.float32)] * 2,
        scratch_shapes=[pltpu.VMEM((2, 2 * dirs * chans, count), jnp.bfloat16)],
        compiler_params=pltpu.CompilerParams(
            dimension_semantics=("arbitrary",), vmem_limit_bytes=40 * 2**20
        ),
        cost_estimate=pl.CostEstimate(flops=flops, bytes_accessed=4 * 2**20, transcendentals=0),
    )(*gains, visibilities, coherencies, stations)


def shards(visibilities, coherencies, start_gains, penalty, stations):
    _, dirs, times, chans, count = start_gains.shape
    half = dirs // 2
    line = lax.axis_size("bl")
    place = lax.axis_index("bl")
    groups = lax.axis_size("chan")
    share = count // line
    basis_table, solved_table = bernstein_tables(chans * groups)
    first_row = lax.axis_index("chan") * chans
    basis = lax.dynamic_slice_in_dim(jnp.asarray(basis_table), first_row, chans, 0)
    solved = lax.dynamic_slice_in_dim(jnp.asarray(solved_table), first_row, chans, 0)
    inner = line // 2 - 1

    def gather_in(values):
        for hop in range(inner):
            values = values + lax.ppermute(values, "bl", [(hop, hop + 1), (line - 1 - hop, line - 2 - hop)])
        return values + lax.ppermute(values, "bl", [(inner, inner + 1), (inner + 1, inner)])

    def spread_out(values):
        for hop in reversed(range(inner)):
            moved = lax.ppermute(values, "bl", [(hop + 1, hop), (line - 2 - hop, line - 1 - hop)])
            values = jnp.where((place == hop) | (place == line - 1 - hop), moved, values)
        return values

    def project(values):
        return jnp.stack([jnp.sum(basis[:, j, None] * values, axis=2) for j in range(POLY)])

    def chan_sum(values):
        step = 1
        while step < groups:
            values = values + lax.ppermute(values, "chan", [(i, i ^ step) for i in range(groups)])
            step *= 2
        return values

    def smooth(sums):
        return sum(solved[:, j, None] * sums[j][:, :, None, :] for j in range(POLY))

    def own(values):
        return lax.dynamic_slice_in_dim(values, place * share, share, values.ndim - 1)

    def update(total, gains, target, weight):
        divisor = total[2] + weight
        return jnp.stack(
            [(total[part] + gains[part] * total[2] + weight * target[part]) / divisor for part in range(2)]
        )

    weights = [penalty[group * half : (group + 1) * half, None, None] for group in range(2)]
    gains = [
        [start_gains[:, group * half : (group + 1) * half, time] for group in range(2)] for time in range(times)
    ]
    targets = gains
    duals = None
    for iteration in range(ITERS):
        sums = [normals(gains[time], visibilities, coherencies, stations, time) for time in range(times)]
        fresh = []
        for time in range(times):
            row = []
            for group in range(2):
                total = gather_in(sums[time][group])
                row.append(spread_out(update(total, gains[time][group], targets[time][group], weights[group])))
            fresh.append(row)
        if iteration < ITERS - 1:
            targets = []
            own_duals = []
            for time in range(times):
                values = jnp.concatenate(fresh[time], axis=1)
                if duals is not None:
                    values = values + duals[time]
                consensus = smooth(chan_sum(project(values)))
                dual = values - consensus
                aim = consensus - dual
                targets.append([aim[:, :half], aim[:, half:]])
                own_duals.append(dual)
            duals = own_duals
        gains = fresh
    whole = jnp.stack([jnp.concatenate(row, axis=1) for row in gains], axis=2)
    consensus = []
    dual = []
    for time in range(times):
        values = own(jnp.concatenate(gains[time], axis=1)) + own(duals[time])
        flat = smooth(chan_sum(project(values)))
        consensus.append(flat)
        dual.append(values - flat)
    return whole, jnp.stack(consensus, axis=2), jnp.stack(dual, axis=2)


def solution(mesh):
    in_specs = (
        P(None, None, "chan", "bl"),
        P(None, None, None, "chan", "bl"),
        P(None, None, None, "chan", None),
        P(),
        P(None, "bl"),
    )
    out_specs = (
        P(None, None, None, "chan", None),
        P(None, None, None, "chan", "bl"),
        P(None, None, None, "chan", "bl"),
    )
    return jax.shard_map(shards, mesh=mesh, in_specs=in_specs, out_specs=out_specs, check_vma=False)
```

```python
import functools
import math

import jax
import jax.numpy as jnp
import numpy as np
from jax import lax
from jax.experimental import pallas as pl
from jax.experimental.pallas import tpu as pltpu
from jax.sharding import PartitionSpec as P

POLY = 4
ITERS = 2
GROUPS = 2
LANES = 128
ROWS_BY_COLS = (((1,), (0,)), ((), ()))
ROWS_BY_ROWS = (((1,), (1,)), ((), ()))
VMEM = pltpu.MemorySpace.VMEM
SMEM = pltpu.MemorySpace.SMEM


def bernstein_tables(total):
    position = (np.arange(total) + 0.5) / total
    basis = np.stack(
        [math.comb(POLY - 1, j) * position**j * (1.0 - position) ** (POLY - 1 - j) for j in range(POLY)], axis=1
    )
    factor = np.linalg.cholesky(basis.T @ basis)
    solved = np.linalg.solve(factor.T, np.linalg.solve(factor, basis.T)).T
    return basis.astype(np.float32), solved.astype(np.float32)


def split(values):
    upper = values.astype(jnp.bfloat16)
    return upper, (values - upper.astype(jnp.float32)).astype(jnp.bfloat16)


def normals_kernel(dirs, chans, line, share, time, start, build, *refs):
    refs = list(refs)
    count = line * share
    half = dirs // GROUPS
    if start:
        place_ref, gain_ref = refs.pop(0), refs.pop(0)
        if share % LANES:
            offsets = [r * share for r in range(line)]
        else:
            offsets = [pl.multiple_of((place_ref[0] ^ r) * share, LANES) for r in range(line)]
        blocks = [
            gain_ref[:, :, time, :, pl.ds(offset, share)].reshape(2 * dirs * chans, share) for offset in offsets
        ]
    else:
        pairs = [(refs.pop(0), refs.pop(0)) for _ in range(GROUPS)]
        blocks = [
            jnp.concatenate(
                [pair[r % 2][r // 2, part] for part in range(2) for pair in pairs], axis=0
            ).reshape(2 * dirs * chans, share)
            for r in range(line)
        ]
    vis_ref, coh_ref, ends_ref = refs[:3]
    outs = refs[3:]
    links = vis_ref.shape[3]
    if build:
        ids = lax.broadcasted_iota(jnp.int32, (count, links), 0)
        pick_ref = outs[2 * GROUPS]
        for end in range(2):
            pick_ref[end] = (ids == ends_ref[end : end + 1, :]).astype(jnp.float32).astype(jnp.bfloat16)
    else:
        pick_ref = ends_ref
    dot = functools.partial(lax.dot_general, preferred_element_type=jnp.float32)
    upper, lower = split(jnp.concatenate(blocks, axis=1))
    first, second = [
        dot(upper, pick_ref[end], ROWS_BY_COLS) + dot(lower, pick_ref[end], ROWS_BY_COLS) for end in range(2)
    ]

    def row(values, part, k):
        begin = (part * dirs + k) * chans
        return values[begin : begin + chans]

    rest_real = vis_ref[0, time]
    rest_imag = vis_ref[1, time]
    sides = []
    for k in range(dirs):
        coh_real = coh_ref[0, k, time].astype(jnp.float32)
        coh_imag = coh_ref[1, k, time].astype(jnp.float32)
        first_real, first_imag = row(first, 0, k), row(first, 1, k)
        second_real, second_imag = row(second, 0, k), row(second, 1, k)
        left_real = second_real * coh_real + second_imag * coh_imag
        left_imag = second_imag * coh_real - second_real * coh_imag
        right_real = first_real * coh_real - first_imag * coh_imag
        right_imag = first_real * coh_imag + first_imag * coh_real
        rest_real = rest_real - (first_real * left_real + first_imag * left_imag)
        rest_imag = rest_imag - (first_imag * left_real - first_real * left_imag)
        sides.append((left_real, left_imag, right_real, right_imag))
    terms = [[], []]
    for group in range(GROUPS):
        chosen = sides[group * half : (group + 1) * half]
        terms[0] += [rest_real * a - rest_imag * b for a, b, _, _ in chosen]
        terms[0] += [rest_real * b + rest_imag * a for a, b, _, _ in chosen]
        terms[0] += [a * a + b * b for a, b, _, _ in chosen]
        terms[1] += [rest_real * c + rest_imag * d for _, _, c, d in chosen]
        terms[1] += [rest_real * d - rest_imag * c for _, _, c, d in chosen]
        terms[1] += [c * c + d * d for _, _, c, d in chosen]
    total = None
    for end in range(2):
        for piece in split(jnp.concatenate(terms[end], axis=0)):
            value = dot(piece, pick_ref[end], ROWS_BY_ROWS)
            total = value if total is None else total + value
    rows = 3 * half * chans
    for group in range(GROUPS):
        for r in range(line):
            piece = total[group * rows : (group + 1) * rows, r * share : (r + 1) * share]
            outs[2 * group + r % 2][r // 2] = piece.reshape(3, half, chans, share)


def normals(gains, start, place, visibilities, coherencies, ends, time, line):
    _, dirs, _, chans, links = coherencies.shape
    build = ends.ndim == 2
    count = gains[0].shape[-1] if start else gains[0].shape[-1] * line
    share = count // line
    half = dirs // GROUPS
    whole = pl.BlockSpec(memory_space=VMEM)
    shape = jax.ShapeDtypeStruct((line // 2, 3, half, chans, share), jnp.float32)
    shapes = [shape] * (2 * GROUPS)
    if build:
        shapes.append(jax.ShapeDtypeStruct((2, count, links), jnp.bfloat16))
    operands = list(gains) + [visibilities, coherencies, ends]
    specs = [whole] * len(operands)
    if start:
        operands.insert(0, place)
        specs.insert(0, pl.BlockSpec(memory_space=SMEM))
    flops = 2 * 2 * 2 * links * count * 5 * dirs * chans
    return pl.pallas_call(
        functools.partial(normals_kernel, dirs, chans, line, share, time, start, build),
        in_specs=specs,
        out_specs=[whole] * len(shapes),
        out_shape=shapes,
        compiler_params=pltpu.CompilerParams(vmem_limit_bytes=40 * 2**20),
        cost_estimate=pl.CostEstimate(flops=flops, bytes_accessed=4 * 2**20, transcendentals=0),
    )(*operands)


def assemble_kernel(times, line, share, place_ref, *refs):
    out_ref = refs[-1]
    half = out_ref.shape[1] // GROUPS
    for time in range(times):
        for group in range(GROUPS):
            for r in range(line):
                source = refs[2 * (time * GROUPS + group) + r % 2]
                offset = pl.multiple_of((place_ref[0] ^ r) * share, LANES)
                out_ref[:, group * half : (group + 1) * half, time, :, pl.ds(offset, share)] = source[r // 2]


def assemble(gains, place, shape, line):
    share = shape[-1] // line
    if share % LANES:
        rows = []
        for row in gains:
            groups = []
            for near, far in row:
                blocks = jnp.stack([near, far], axis=1).reshape((line,) + near.shape[1:])
                parts = [lax.dynamic_index_in_dim(blocks, place[0] ^ r, 0, False) for r in range(line)]
                groups.append(jnp.concatenate(parts, axis=-1))
            rows.append(jnp.concatenate(groups, axis=1))
        return jnp.stack(rows, axis=2)
    flat = [block for row in gains for pair in row for block in pair]
    whole = pl.BlockSpec(memory_space=VMEM)
    return pl.pallas_call(
        functools.partial(assemble_kernel, shape[2], line, share),
        in_specs=[pl.BlockSpec(memory_space=SMEM)] + [whole] * len(flat),
        out_specs=whole,
        out_shape=jax.ShapeDtypeStruct(shape, jnp.float32),
        compiler_params=pltpu.CompilerParams(vmem_limit_bytes=16 * 2**20),
    )(place, *flat)


def shards(visibilities, coherencies, start_gains, penalty, stations):
    _, dirs, times, chans, count = start_gains.shape
    half = dirs // GROUPS
    line = lax.axis_size("bl")
    index = lax.axis_index("bl")
    place = index.astype(jnp.int32).reshape(1)
    groups = lax.axis_size("chan")
    share = count // line
    basis_table, solved_table = bernstein_tables(chans * groups)
    first_row = lax.axis_index("chan") * chans
    basis = lax.dynamic_slice_in_dim(jnp.asarray(basis_table), first_row, chans, 0)
    solved = lax.dynamic_slice_in_dim(jnp.asarray(solved_table), first_row, chans, 0)
    relative = ((stations // share) ^ index) * share + stations % share

    def swap(values, axis, size, bit):
        return lax.ppermute(values, axis, [(i, i ^ bit) for i in range(size)])

    def sum_own(keep, send):
        bit = 1
        while True:
            got = swap(send, "bl", line, bit)
            if keep.shape[0] == 1:
                return keep[0] + got[0]
            both = keep + got
            keep, send = both[0::2], both[1::2]
            bit *= 2

    def spread(own):
        blocks = own[None]
        bit = line // 2
        while bit > 1:
            got = swap(blocks, "bl", line, bit)
            blocks = jnp.stack([blocks, got], axis=1).reshape((2 * blocks.shape[0],) + blocks.shape[1:])
            bit //= 2
        return blocks, swap(blocks, "bl", line, 1)

    def project(values):
        return jnp.stack([jnp.sum(basis[:, j, None] * values, axis=2) for j in range(POLY)])

    def chan_sum(values):
        bit = 1
        while bit < groups:
            values = values + swap(values, "chan", groups, bit)
            bit *= 2
        return values

    def smooth(sums):
        return sum(solved[:, j, None] * sums[j][:, :, None, :] for j in range(POLY))

    def update(total, gains, target, weight):
        divisor = total[2] + weight
        return jnp.stack(
            [(total[part] + gains[part] * total[2] + weight * target[part]) / divisor for part in range(2)]
        )

    weights = [penalty[group * half : (group + 1) * half, None, None] for group in range(GROUPS)]
    ordered = start_gains
    if share % LANES:
        parts = [lax.dynamic_slice_in_dim(start_gains, (index ^ r) * share, share, 4) for r in range(line)]
        ordered = jnp.concatenate(parts, axis=4)
    own_start = lax.dynamic_slice_in_dim(start_gains, index * share, share, 4)
    own = [
        [own_start[:, group * half : (group + 1) * half, time] for group in range(GROUPS)] for time in range(times)
    ]
    targets = own
    duals = None
    gains = None
    picks = None
    for iteration in range(ITERS):
        sums = []
        for time in range(times):
            if iteration == 0:
                out = normals(
                    [ordered], True, place, visibilities, coherencies, relative if time == 0 else picks, time, line
                )
                picks = out[2 * GROUPS] if time == 0 else picks
            else:
                flat = [block for pair in gains[time] for block in pair]
                out = normals(flat, False, place, visibilities, coherencies, picks, time, line)
            sums.append(out)
        fresh = []
        gains = []
        for time in range(times):
            fresh.append([])
            gains.append([])
            for group in range(GROUPS):
                total = sum_own(sums[time][2 * group], sums[time][2 * group + 1])
                value = update(total, own[time][group], targets[time][group], weights[group])
                fresh[time].append(value)
                gains[time].append(spread(value))
        own = fresh
        values = [jnp.concatenate(row, axis=1) for row in own]
        if duals is not None:
            values = [value + dual for value, dual in zip(values, duals)]
        sums = chan_sum(jnp.stack([project(value) for value in values]))
        consensus = [smooth(sums[time]) for time in range(times)]
        duals = [value - flat for value, flat in zip(values, consensus)]
        targets = [
            [(flat - dual)[:, group * half : (group + 1) * half] for group in range(GROUPS)]
            for flat, dual in zip(consensus, duals)
        ]
    return (
        assemble(gains, place, start_gains.shape, line),
        jnp.stack(consensus, axis=2),
        jnp.stack(duals, axis=2),
    )


def solution(mesh):
    in_specs = (
        P(None, None, "chan", "bl"),
        P(None, None, None, "chan", "bl"),
        P(None, None, None, "chan", None),
        P(),
        P(None, "bl"),
    )
    out_specs = (
        P(None, None, None, "chan", None),
        P(None, None, None, "chan", "bl"),
        P(None, None, None, "chan", "bl"),
    )
    return jax.shard_map(shards, mesh=mesh, in_specs=in_specs, out_specs=out_specs, check_vma=False)
```

```python
import functools
import math

import jax
import jax.numpy as jnp
import numpy as np
from jax import lax
from jax.experimental import pallas as pl
from jax.experimental.pallas import tpu as pltpu
from jax.sharding import PartitionSpec as P

POLY = 4
ITERS = 2
LANES = 128
SUBLANES = 8
DIRECT_SUM = False
EARLY = False
STEP_BEFORE = 99
DIRECT_SPREAD = (False, False)
CHUNKING = "times"
ROWS_BY_COLS = (((1,), (0,)), ((), ()))
ROWS_BY_ROWS = (((1,), (1,)), ((), ()))
VMEM = pltpu.MemorySpace.VMEM
HBM = pltpu.MemorySpace.HBM
WHOLE = pl.BlockSpec(memory_space=VMEM)
OUTSIDE = pl.BlockSpec(memory_space=pl.ANY)
SCALARS = pl.BlockSpec(memory_space=pltpu.MemorySpace.SMEM)
CHEAP = pl.CostEstimate(flops=2**20, bytes_accessed=2**10, transcendentals=0)


def run(kernel, token, in_specs, out_shape, operands, scratch=(), limit=4):
    count = len(token)
    return pl.pallas_call(
        lambda *refs: kernel(*refs[count:]),
        in_specs=[OUTSIDE] * count + list(in_specs),
        out_specs=[WHOLE] * len(out_shape),
        out_shape=list(out_shape),
        scratch_shapes=list(scratch),
        compiler_params=pltpu.CompilerParams(vmem_limit_bytes=limit * 2**20),
        cost_estimate=CHEAP,
    )(*token, *operands)


def bernstein_tables(total):
    position = (np.arange(total) + 0.5) / total
    basis = np.stack(
        [math.comb(POLY - 1, j) * position**j * (1.0 - position) ** (POLY - 1 - j) for j in range(POLY)], axis=1
    )
    factor = np.linalg.cholesky(basis.T @ basis)
    solved = np.linalg.solve(factor.T, np.linalg.solve(factor, basis.T)).T
    return basis.astype(np.float32), solved.astype(np.float32)


def split(values):
    upper = values.astype(jnp.bfloat16)
    return upper, (values - upper.astype(jnp.float32)).astype(jnp.bfloat16)


def chunks_of(times, chans):
    if CHUNKING == "channels" and chans % SUBLANES == 0:
        return [(0, times, f, f + SUBLANES) for f in range(0, chans, SUBLANES)]
    return [(t, t + 1, 0, chans) for t in range(times)]


def block_of(refs, r):
    return refs[r % 2][r // 2] if len(refs) == 2 else refs[r][0]


def normals_kernel(chunk, line, share, start, fill, sources, *refs):
    t0, t1, f0, f1 = chunk
    refs = list(refs)
    place_ref = refs.pop(0)
    gain_refs = [refs.pop(0) for _ in range(sources)]
    vis_ref, coh_ref, pick_ref = [refs.pop(0) for _ in range(3)]
    outs = [refs.pop(0) for _ in range(line if DIRECT_SUM else 2)]
    own_ref = refs.pop(0) if start else None
    dirs, links = coh_ref.shape[1], coh_ref.shape[4]
    rows = (t1 - t0) * (f1 - f0)
    offsets = [(place_ref[0] ^ r) * share for r in range(line)]
    copies = []
    if fill:
        station_hbm, pick_ref = pick_ref, refs.pop(0)
        station_ref, sems = refs[-2:]
        pairs = [(station_hbm, station_ref)]
        for t in range(vis_ref.shape[1]):
            pairs += [
                (gain_refs[0].at[:, :, t], refs[0].at[:, :, t]),
                (vis_ref.at[:, t], refs[1].at[:, t]),
                (coh_ref.at[:, :, t], refs[2].at[:, :, t]),
            ]
        gain_refs, vis_ref, coh_ref = [refs[0]], refs[1], refs[2]
        copies = [pltpu.make_async_copy(src, dst, sems.at[i]) for i, (src, dst) in enumerate(pairs)]
        for copy in copies:
            copy.start()
        copies[0].wait()
        build_picks(line, share, offsets, station_ref, pick_ref)
        for t in range(t0, t1):
            copies[1 + 3 * t].wait()
    if start:
        if share % LANES:
            offsets = [r * share for r in range(line)]
        else:
            offsets = [pl.multiple_of(offset, LANES) for offset in offsets]
        blocks = [gain_refs[0][:, :, t0:t1, f0:f1, pl.ds(offset, share)] for offset in offsets]
        own_ref[...] = blocks[0]
    else:
        blocks = [block_of(gain_refs, r) for r in range(line)]
    blocks = [block.reshape(2 * dirs * rows, share) for block in blocks]
    dot = functools.partial(lax.dot_general, preferred_element_type=jnp.float32)
    upper, lower = split(jnp.concatenate(blocks, axis=1))
    first, second = [
        dot(upper, pick_ref[end], ROWS_BY_COLS) + dot(lower, pick_ref[end], ROWS_BY_COLS) for end in range(2)
    ]

    def row(values, part, k):
        begin = (part * dirs + k) * rows
        return values[begin : begin + rows]

    def coherency(part, k):
        low = f0 // 16 * 16
        high = min(-(-f1 // 16) * 16, coh_ref.shape[3])
        values = coh_ref[part, k, t0:t1, low:high].astype(jnp.float32)
        return values[:, f0 - low : f1 - low].reshape(rows, links)

    for t in range(t0, t1 if fill else t0):
        copies[2 + 3 * t].wait()
        copies[3 + 3 * t].wait()
    rest_real = vis_ref[0, t0:t1, f0:f1].reshape(rows, links)
    rest_imag = vis_ref[1, t0:t1, f0:f1].reshape(rows, links)
    sides = []
    for k in range(dirs):
        coh_real, coh_imag = coherency(0, k), coherency(1, k)
        first_real, first_imag = row(first, 0, k), row(first, 1, k)
        second_real, second_imag = row(second, 0, k), row(second, 1, k)
        left_real = second_real * coh_real + second_imag * coh_imag
        left_imag = second_imag * coh_real - second_real * coh_imag
        right_real = first_real * coh_real - first_imag * coh_imag
        right_imag = first_real * coh_imag + first_imag * coh_real
        rest_real = rest_real - (first_real * left_real + first_imag * left_imag)
        rest_imag = rest_imag - (first_imag * left_real - first_real * left_imag)
        sides.append((left_real, left_imag, right_real, right_imag))
    terms = [[], []]
    terms[0] += [rest_real * a - rest_imag * b for a, b, _, _ in sides]
    terms[0] += [rest_real * b + rest_imag * a for a, b, _, _ in sides]
    terms[0] += [a * a + b * b for a, b, _, _ in sides]
    terms[1] += [rest_real * c + rest_imag * d for _, _, c, d in sides]
    terms[1] += [rest_real * d - rest_imag * c for _, _, c, d in sides]
    terms[1] += [c * c + d * d for _, _, c, d in sides]
    total = None
    for end in range(2):
        for piece in split(jnp.concatenate(terms[end], axis=0)):
            value = dot(piece, pick_ref[end], ROWS_BY_ROWS)
            total = value if total is None else total + value
    for r in range(line):
        piece = total[:, r * share : (r + 1) * share].reshape(3, dirs, t1 - t0, f1 - f0, share)
        if DIRECT_SUM:
            outs[r][0] = piece
        else:
            outs[r % 2][r // 2] = piece
    for t in range(vis_ref.shape[1] if fill else 0):
        if not t0 <= t < t1:
            for copy in copies[1 + 3 * t : 4 + 3 * t]:
                copy.wait()


def build_picks(line, share, offsets, station_ref, pick_ref):
    links = station_ref.shape[1]
    one, zero = jnp.ones((), jnp.bfloat16), jnp.zeros((), jnp.bfloat16)
    ids = lax.broadcasted_iota(jnp.int32, (share, links), 0).astype(jnp.float32).astype(jnp.bfloat16)
    for end in range(2):
        for r in range(line):
            number = station_ref[end : end + 1, :] - offsets[r]
            number = jnp.where((number >= 0) & (number < share), number, -1)
            number = number.astype(jnp.float32).astype(jnp.bfloat16)
            pick_ref[end, r * share : (r + 1) * share] = jnp.where(ids == number, one, zero)


def picks_kernel(line, share, place_ref, station_ref, pick_ref):
    offsets = [(place_ref[0] ^ r) * share for r in range(line)]
    build_picks(line, share, offsets, station_ref, pick_ref)


def make_picks(line, count, place, stations, token):
    shapes = [VMEM((2, count, stations.shape[1]), jnp.bfloat16)]
    kernel = functools.partial(picks_kernel, line, count // line)
    return run(kernel, token, [SCALARS, WHOLE], shapes, [place, stations], (), 8)[0]


def normals(chunk, line, start, fill, place, gains, visibilities, coherencies, picks, token):
    t0, t1, f0, f1 = chunk
    dirs, links = coherencies.shape[1], coherencies.shape[4]
    count = gains[0].shape[-1] if start else gains[0].shape[-1] * line
    share = count // line
    piece = (dirs, t1 - t0, f1 - f0, share)
    lead = [1] * line if DIRECT_SUM else [line // 2] * 2
    shapes = [jax.ShapeDtypeStruct((n, 3) + piece, jnp.float32) for n in lead]
    scratch = []
    if start:
        shapes.append(jax.ShapeDtypeStruct((2,) + piece, jnp.float32))
    if fill:
        shapes.append(VMEM((2, count, links), jnp.bfloat16))
        times = visibilities.shape[1]
        scratch = [pltpu.VMEM((2, links), jnp.int32), pltpu.SemaphoreType.DMA((1 + 3 * times,))]
        shapes += [VMEM(x.shape, x.dtype) for x in (gains[0], visibilities, coherencies)]
    spaces = [HBM if fill else VMEM] * (len(gains) + 3)
    sources = [*gains, visibilities, coherencies, picks]
    sources = [pltpu.with_memory_space_constraint(x, space) for x, space in zip(sources, spaces)]
    specs = [OUTSIDE if space is HBM else WHOLE for space in spaces]
    kernel = functools.partial(normals_kernel, chunk, line, share, start, fill, len(gains))
    return run(kernel, token, [SCALARS] + specs, shapes, [place, *sources], scratch, 32)


def add_kernel(keep_ref, got_ref, own_ref, send_ref):
    for i in range(own_ref.shape[0]):
        own_ref[i] = keep_ref[2 * i] + got_ref[2 * i]
        send_ref[i] = keep_ref[2 * i + 1] + got_ref[2 * i + 1]


def add_parts(keep, got, token):
    shape = jax.ShapeDtypeStruct((keep.shape[0] // 2,) + keep.shape[1:], keep.dtype)
    return run(add_kernel, token, [WHOLE] * 2, [shape] * 2, [keep, got])


def update_kernel(chunk, parts, first, chans, penalty_ref, place_ref, basis_ref, before_ref, *refs):
    t0, t1, f0, f1 = chunk
    part_refs = refs[:parts]
    extra = refs[parts:-2]
    new_ref, sum_ref = refs[-2:]
    sum_ref[...] = before_ref[...]
    basis = basis_ref[pl.ds(place_ref[1] * chans + f0, f1 - f0)]
    for k in range(new_ref.shape[1]):
        load = penalty_ref[k]
        for t in range(t0, t1):
            weight = sum(ref[0, 2, k, t - t0] for ref in part_refs)
            divisor = weight + load
            for part in range(2):
                gain = extra[0][part, k, t - t0]
                target = gain if first else extra[1][part, k, t, f0:f1]
                total = sum(ref[0, part, k, t - t0] for ref in part_refs)
                new = (total + gain * weight + load * target) / divisor
                new_ref[part, k, t - t0] = new
                value = new if first else new + extra[2][part, k, t, f0:f1]
                for j in range(POLY):
                    row = jnp.sum(basis[:, j : j + 1] * value, axis=0, keepdims=True)
                    sum_ref[t, j, part, k : k + 1] += row


def update(chunk, first, chans, penalty, place, basis, before, parts, extra, token):
    shapes = [
        jax.ShapeDtypeStruct((2,) + parts[0].shape[2:], jnp.float32),
        jax.ShapeDtypeStruct(before.shape, jnp.float32),
    ]
    operands = [basis, before, *parts, *extra]
    kernel = functools.partial(update_kernel, chunk, len(parts), first, chans)
    return run(kernel, token, [SCALARS] * 2 + [WHOLE] * len(operands), shapes, [penalty, place, *operands])


def smooth_kernel(chunks, first, chans, place_ref, solved_ref, sum_ref, *refs):
    one_ref, two_ref = refs[-2:]
    solved = solved_ref[pl.ds(place_ref[1] * chans, chans)]
    for (t0, t1, f0, f1), gain_ref in zip(chunks, refs):
        for part in range(2):
            for k in range(one_ref.shape[1]):
                for t in range(t0, t1):
                    flat = sum(
                        solved[f0:f1, j : j + 1] * sum_ref[t, j, part, k : k + 1] for j in range(POLY)
                    )
                    value = gain_ref[part, k, t - t0]
                    at = (part, k, t, slice(f0, f1))
                    if first:
                        dual = value - flat
                        one_ref[at] = flat - dual
                    else:
                        dual = refs[len(chunks)][at] + value - flat
                        one_ref[at] = flat
                    two_ref[at] = dual


def smooth(chunks, first, place, solved, sums, gains, extra, dims, token):
    operands = [solved, sums, *gains, *extra]
    shapes = [jax.ShapeDtypeStruct(dims, jnp.float32)] * 2
    kernel = functools.partial(smooth_kernel, chunks, first, dims[3])
    return run(kernel, token, [SCALARS] + [WHOLE] * len(operands), shapes, [place, *operands])


def assemble_kernel(chunks, line, share, place_ref, *refs):
    out_ref = refs[-1]
    each = (len(refs) - 1) // len(chunks)
    for i, (t0, t1, f0, f1) in enumerate(chunks):
        for r in range(line):
            offset = pl.multiple_of((place_ref[0] ^ r) * share, LANES)
            out_ref[:, :, t0:t1, f0:f1, pl.ds(offset, share)] = block_of(refs[i * each : (i + 1) * each], r)


def assemble(chunks, line, place, gains, dims):
    share = dims[-1] // line
    if share % LANES:
        whole = jnp.zeros(dims, jnp.float32)
        for (t0, t1, f0, f1), blocks in zip(chunks, gains):
            stacked = jnp.stack([block_of(blocks, r) for r in range(line)])
            parts = [lax.dynamic_index_in_dim(stacked, place[0] ^ r, 0, False) for r in range(line)]
            whole = whole.at[:, :, t0:t1, f0:f1].set(jnp.concatenate(parts, axis=-1))
        return whole
    flat = [block for blocks in gains for block in blocks]
    kernel = functools.partial(assemble_kernel, chunks, line, share)
    shapes = [jax.ShapeDtypeStruct(dims, jnp.float32)]
    return run(kernel, [], [SCALARS] + [WHOLE] * len(flat), shapes, [place, *flat])[0]


def shards(visibilities, coherencies, start_gains, penalty, stations):
    dims = start_gains.shape
    _, dirs, times, chans, count = dims
    line = lax.axis_size("bl")
    index = lax.axis_index("bl")
    place = jnp.stack([index, lax.axis_index("chan")]).astype(jnp.int32)
    groups = lax.axis_size("chan")
    share = count // line
    basis, solved = [jnp.asarray(table) for table in bernstein_tables(chans * groups)]

    def swap(values, axis, size, bit):
        return lax.ppermute(values, axis, [(i, i ^ bit) for i in range(size)])

    def chan_steps(values):
        steps = [values]
        bit = 1
        while bit < groups:
            steps.append(steps[-1] + swap(steps[-1], "chan", groups, bit))
            bit *= 2
        return steps

    ordered = start_gains
    if share % LANES:
        parts = [lax.dynamic_slice_in_dim(start_gains, (index ^ r) * share, share, 4) for r in range(line)]
        ordered = jnp.concatenate(parts, axis=4)
    own_dims = dims[:4] + (share,)
    chunks = chunks_of(times, chans)
    token = []
    gains = own = targets = duals = projected = None

    def spread(values, direct):
        blocks, bit, arrived = values[None], line // 2, None
        if direct:
            blocks = [blocks] + [swap(blocks, "bl", line, r) for r in range(1, line)]
            return blocks, blocks[1]
        while bit > 1:
            got = swap(blocks, "bl", line, bit)
            arrived = got if arrived is None else arrived
            blocks = jnp.stack([blocks, got], axis=1).reshape((2 * blocks.shape[0],) + blocks.shape[1:])
            bit //= 2
        return [blocks, swap(blocks, "bl", line, 1)], arrived

    for iteration in range(ITERS):
        first = iteration == 0
        parts, fresh = [], []
        if not first:
            picks = make_picks(line, count, place, stations, token)
            token = [picks]
            steps = chan_steps(projected)
        for c, chunk in enumerate(chunks):
            fill = first and c == 0
            if not first and c + STEP_BEFORE < len(steps):
                token = token + [steps[c + STEP_BEFORE]]
            out = normals(
                chunk,
                line,
                first,
                fill,
                place,
                [ordered] if first else gains[c],
                visibilities,
                coherencies,
                stations if fill else picks,
                token,
            )
            token = [out[0]]
            count_sent = line if DIRECT_SUM else 2
            if DIRECT_SUM:
                parts.append([out[0]] + [swap(out[r], "bl", line, r) for r in range(1, line)])
            else:
                parts.append([out[0], swap(out[1], "bl", line, 1)])
            rest = list(out[count_sent:])
            if first:
                fresh.append(rest.pop(0))
            if fill:
                picks, ordered, visibilities, coherencies = rest
        if first:
            own = fresh
        else:
            targets, duals = smooth(chunks, True, place, solved, steps[-1], own, [], own_dims, [])
        bit = 2
        while bit < line and not DIRECT_SUM:
            for c in range(len(chunks)):
                keep, send = add_parts(*parts[c], token)
                parts[c] = [keep, swap(send, "bl", line, bit)]
                token = [keep]
            bit *= 2
        gains, fresh = [], []
        projected = jnp.zeros((times, POLY, 2, dirs, share), jnp.float32)
        for c, chunk in enumerate(chunks):
            extra = [own[c]] if first else [own[c], targets, duals]
            new, projected = update(chunk, first, chans, penalty, place, basis, projected, parts[c], extra, token)
            pair, arrived = spread(new, DIRECT_SPREAD[iteration])
            token = [new] if first or not EARLY else [new, arrived]
            gains.append(pair)
            fresh.append(new)
        own = fresh
    steps = chan_steps(projected)
    consensus, dual = smooth(chunks, False, place, solved, steps[-1], own, [duals], own_dims, [])
    return assemble(chunks, line, place, gains, dims), consensus, dual


def solution(mesh):
    in_specs = (
        P(None, None, "chan", "bl"),
        P(None, None, None, "chan", "bl"),
        P(None, None, None, "chan", None),
        P(),
        P(None, "bl"),
    )
    out_specs = (
        P(None, None, None, "chan", None),
        P(None, None, None, "chan", "bl"),
        P(None, None, None, "chan", "bl"),
    )
    return jax.shard_map(shards, mesh=mesh, in_specs=in_specs, out_specs=out_specs, check_vma=False)
```

```python
import functools
import math

import jax
import jax.numpy as jnp
import numpy as np
from jax import lax
from jax.experimental import pallas as pl
from jax.experimental.pallas import tpu as pltpu
from jax.sharding import PartitionSpec as P

POLY = 4
ITERS = 2
LANES = 128
SUBLANES = 8
JOIN_AFTER = ((0, 0), (1, 2))
ADD_AFTER = 2
ROWS_BY_COLS = (((1,), (0,)), ((), ()))
ROWS_BY_ROWS = (((1,), (1,)), ((), ()))
VMEM = pltpu.MemorySpace.VMEM
HBM = pltpu.MemorySpace.HBM
WHOLE = pl.BlockSpec(memory_space=VMEM)
OUTSIDE = pl.BlockSpec(memory_space=pl.ANY)
SCALARS = pl.BlockSpec(memory_space=pltpu.MemorySpace.SMEM)
CHEAP = pl.CostEstimate(flops=2**20, bytes_accessed=2**10, transcendentals=0)


def run(kernel, token, in_specs, out_shape, operands, scratch=(), limit=4):
    count = len(token)
    return pl.pallas_call(
        lambda *refs: kernel(*refs[count:]),
        in_specs=[OUTSIDE] * count + list(in_specs),
        out_specs=[WHOLE] * len(out_shape),
        out_shape=list(out_shape),
        scratch_shapes=list(scratch),
        compiler_params=pltpu.CompilerParams(vmem_limit_bytes=limit * 2**20),
        cost_estimate=CHEAP,
    )(*token, *operands)


def bernstein_tables(total):
    position = (np.arange(total) + 0.5) / total
    basis = np.stack(
        [math.comb(POLY - 1, j) * position**j * (1.0 - position) ** (POLY - 1 - j) for j in range(POLY)], axis=1
    )
    factor = np.linalg.cholesky(basis.T @ basis)
    solved = np.linalg.solve(factor.T, np.linalg.solve(factor, basis.T)).T
    return basis.astype(np.float32), solved.astype(np.float32)


def split(values):
    upper = values.astype(jnp.bfloat16)
    return upper, (values - upper.astype(jnp.float32)).astype(jnp.bfloat16)


def chunks_of(times, chans):
    return [(t, t + 1, 0, chans) for t in range(times)]


def block_of(refs, r):
    return refs[r % 2][r // 2] if len(refs) == 2 else refs[r][0]


def normals_kernel(chunk, line, share, start, fill, sources, *refs):
    t0, t1, f0, f1 = chunk
    refs = list(refs)
    place_ref = refs.pop(0)
    gain_refs = [refs.pop(0) for _ in range(sources)]
    vis_ref, coh_ref, pick_ref = [refs.pop(0) for _ in range(3)]
    outs = [refs.pop(0) for _ in range(2)]
    own_ref = refs.pop(0) if start else None
    dirs, links = coh_ref.shape[1], coh_ref.shape[4]
    rows = (t1 - t0) * (f1 - f0)
    offsets = [(place_ref[0] ^ r) * share for r in range(line)]
    copies = []
    if fill:
        station_hbm, pick_ref = pick_ref, refs.pop(0)
        station_ref, sems = refs[-2:]
        pairs = [(station_hbm, station_ref)]
        for t in range(vis_ref.shape[1]):
            pairs += [
                (gain_refs[0].at[:, :, t], refs[0].at[:, :, t]),
                (vis_ref.at[:, t], refs[1].at[:, t]),
                (coh_ref.at[:, :, t], refs[2].at[:, :, t]),
            ]
        gain_refs, vis_ref, coh_ref = [refs[0]], refs[1], refs[2]
        copies = [pltpu.make_async_copy(src, dst, sems.at[i]) for i, (src, dst) in enumerate(pairs)]
        for copy in copies:
            copy.start()
        copies[0].wait()
        for t in range(t0, t1):
            copies[1 + 3 * t].wait()
        build_picks(line, share, offsets, station_ref, pick_ref)
    if start:
        if share % LANES:
            offsets = [r * share for r in range(line)]
        else:
            offsets = [pl.multiple_of(offset, LANES) for offset in offsets]
        blocks = [gain_refs[0][:, :, t0:t1, f0:f1, pl.ds(offset, share)] for offset in offsets]
        own_ref[...] = blocks[0]
    else:
        blocks = [block_of(gain_refs, r) for r in range(line)]
    blocks = [block.reshape(2 * dirs * rows, share) for block in blocks]
    dot = functools.partial(lax.dot_general, preferred_element_type=jnp.float32)
    both = jnp.concatenate(split(jnp.concatenate(blocks, axis=1)), axis=0)
    wide = [dot(both, pick_ref[end], ROWS_BY_COLS) for end in range(2)]
    height = 2 * dirs * rows
    first, second = [values[:height] + values[height:] for values in wide]

    def row(values, part, k):
        begin = (part * dirs + k) * rows
        return values[begin : begin + rows]

    def coherency(part, k):
        low = f0 // 16 * 16
        high = min(-(-f1 // 16) * 16, coh_ref.shape[3])
        values = coh_ref[part, k, t0:t1, low:high].astype(jnp.float32)
        return values[:, f0 - low : f1 - low].reshape(rows, links)

    for t in range(t0, t1 if fill else t0):
        copies[2 + 3 * t].wait()
        copies[3 + 3 * t].wait()
    rest_real = vis_ref[0, t0:t1, f0:f1].reshape(rows, links)
    rest_imag = vis_ref[1, t0:t1, f0:f1].reshape(rows, links)
    sides = []
    for k in range(dirs):
        coh_real, coh_imag = coherency(0, k), coherency(1, k)
        first_real, first_imag = row(first, 0, k), row(first, 1, k)
        second_real, second_imag = row(second, 0, k), row(second, 1, k)
        left_real = second_real * coh_real + second_imag * coh_imag
        left_imag = second_imag * coh_real - second_real * coh_imag
        right_real = first_real * coh_real - first_imag * coh_imag
        right_imag = first_real * coh_imag + first_imag * coh_real
        rest_real = rest_real - (first_real * left_real + first_imag * left_imag)
        rest_imag = rest_imag - (first_imag * left_real - first_real * left_imag)
        sides.append((left_real, left_imag, right_real, right_imag))
    terms = [[], []]
    terms[0] += [rest_real * a - rest_imag * b for a, b, _, _ in sides]
    terms[0] += [rest_real * b + rest_imag * a for a, b, _, _ in sides]
    terms[0] += [a * a + b * b for a, b, _, _ in sides]
    terms[1] += [rest_real * c + rest_imag * d for _, _, c, d in sides]
    terms[1] += [rest_real * d - rest_imag * c for _, _, c, d in sides]
    terms[1] += [c * c + d * d for _, _, c, d in sides]
    pieces = [split(jnp.concatenate(terms[end], axis=0)) for end in range(2)]
    wide = jnp.concatenate([pick_ref[0], pick_ref[1]], axis=1)
    total = None
    for part in range(2):
        value = dot(jnp.concatenate([pieces[0][part], pieces[1][part]], axis=1), wide, ROWS_BY_ROWS)
        total = value if total is None else total + value
    for r in range(line):
        piece = total[:, r * share : (r + 1) * share].reshape(3, dirs, t1 - t0, f1 - f0, share)
        outs[r % 2][r // 2] = piece
    for t in range(vis_ref.shape[1] if fill else 0):
        if not t0 <= t < t1:
            for copy in copies[1 + 3 * t : 4 + 3 * t]:
                copy.wait()


def build_picks(line, share, offsets, station_ref, pick_ref):
    links = station_ref.shape[1]
    one, zero = jnp.ones((), jnp.bfloat16), jnp.zeros((), jnp.bfloat16)
    ids = lax.broadcasted_iota(jnp.int32, (share, links), 0).astype(jnp.float32).astype(jnp.bfloat16)
    for end in range(2):
        for r in range(line):
            number = station_ref[end : end + 1, :] - offsets[r]
            number = jnp.where((number >= 0) & (number < share), number, -1)
            number = number.astype(jnp.float32).astype(jnp.bfloat16)
            pick_ref[end, r * share : (r + 1) * share] = jnp.where(ids == number, one, zero)


def picks_kernel(line, share, place_ref, station_ref, pick_ref):
    offsets = [(place_ref[0] ^ r) * share for r in range(line)]
    build_picks(line, share, offsets, station_ref, pick_ref)


def make_picks(line, count, place, stations, token):
    shapes = [VMEM((2, count, stations.shape[1]), jnp.bfloat16)]
    kernel = functools.partial(picks_kernel, line, count // line)
    return run(kernel, token, [SCALARS, WHOLE], shapes, [place, stations], (), 8)[0]


def normals(chunk, line, start, fill, place, gains, visibilities, coherencies, picks, token):
    t0, t1, f0, f1 = chunk
    dirs, links = coherencies.shape[1], coherencies.shape[4]
    count = gains[0].shape[-1] if start else gains[0].shape[-1] * line
    share = count // line
    piece = (dirs, t1 - t0, f1 - f0, share)
    shapes = [jax.ShapeDtypeStruct((line // 2, 3) + piece, jnp.float32)] * 2
    scratch = []
    if start:
        shapes.append(jax.ShapeDtypeStruct((2,) + piece, jnp.float32))
    if fill:
        shapes.append(VMEM((2, count, links), jnp.bfloat16))
        times = visibilities.shape[1]
        scratch = [pltpu.VMEM((2, links), jnp.int32), pltpu.SemaphoreType.DMA((1 + 3 * times,))]
        shapes += [VMEM(x.shape, x.dtype) for x in (gains[0], visibilities, coherencies)]
    spaces = [HBM if fill else VMEM] * (len(gains) + 3)
    sources = [*gains, visibilities, coherencies, picks]
    sources = [pltpu.with_memory_space_constraint(x, space) for x, space in zip(sources, spaces)]
    specs = [OUTSIDE if space is HBM else WHOLE for space in spaces]
    kernel = functools.partial(normals_kernel, chunk, line, share, start, fill, len(gains))
    return run(kernel, token, [SCALARS] + specs, shapes, [place, *sources], scratch, 32)


def add_kernel(keep_ref, got_ref, own_ref, send_ref):
    for i in range(own_ref.shape[0]):
        own_ref[i] = keep_ref[2 * i] + got_ref[2 * i]
        send_ref[i] = keep_ref[2 * i + 1] + got_ref[2 * i + 1]


def add_parts(keep, got, token):
    shape = jax.ShapeDtypeStruct((keep.shape[0] // 2,) + keep.shape[1:], keep.dtype)
    return run(add_kernel, token, [WHOLE] * 2, [shape] * 2, [keep, got])


def join_kernel(blocks_ref, got_ref, out_ref):
    for i in range(blocks_ref.shape[0]):
        out_ref[2 * i] = blocks_ref[i]
        out_ref[2 * i + 1] = got_ref[i]


def join(blocks, got, token):
    shape = jax.ShapeDtypeStruct((2 * blocks.shape[0],) + blocks.shape[1:], blocks.dtype)
    return run(join_kernel, token, [WHOLE] * 2, [shape], [blocks, got])[0]


def update_kernel(chunk, parts, first, chans, penalty_ref, place_ref, basis_ref, before_ref, *refs):
    t0, t1, f0, f1 = chunk
    part_refs = refs[:parts]
    extra = refs[parts:-2]
    new_ref, sum_ref = refs[-2:]
    sum_ref[...] = before_ref[...]
    basis = basis_ref[pl.ds(place_ref[1] * chans + f0, f1 - f0)]
    for k in range(new_ref.shape[1]):
        load = penalty_ref[k]
        for t in range(t0, t1):
            weight = sum(ref[0, 2, k, t - t0] for ref in part_refs)
            divisor = weight + load
            for part in range(2):
                gain = extra[0][part, k, t - t0]
                target = gain if first else extra[1][part, k, t, f0:f1]
                total = sum(ref[0, part, k, t - t0] for ref in part_refs)
                new = (total + gain * weight + load * target) / divisor
                new_ref[part, k, t - t0] = new
                value = new if first else new + extra[2][part, k, t, f0:f1]
                for j in range(POLY):
                    row = jnp.sum(basis[:, j : j + 1] * value, axis=0, keepdims=True)
                    sum_ref[t, j, part, k : k + 1] += row


def update(chunk, first, chans, penalty, place, basis, before, parts, extra, token):
    shapes = [
        jax.ShapeDtypeStruct((2,) + parts[0].shape[2:], jnp.float32),
        jax.ShapeDtypeStruct(before.shape, jnp.float32),
    ]
    operands = [basis, before, *parts, *extra]
    kernel = functools.partial(update_kernel, chunk, len(parts), first, chans)
    return run(kernel, token, [SCALARS] * 2 + [WHOLE] * len(operands), shapes, [penalty, place, *operands])


def smooth_kernel(chunks, first, chans, place_ref, solved_ref, sum_ref, *refs):
    one_ref, two_ref = refs[-2:]
    solved = solved_ref[pl.ds(place_ref[1] * chans, chans)]
    for (t0, t1, f0, f1), gain_ref in zip(chunks, refs):
        for part in range(2):
            for k in range(one_ref.shape[1]):
                for t in range(t0, t1):
                    flat = sum(
                        solved[f0:f1, j : j + 1] * sum_ref[t, j, part, k : k + 1] for j in range(POLY)
                    )
                    value = gain_ref[part, k, t - t0]
                    at = (part, k, t, slice(f0, f1))
                    if first:
                        dual = value - flat
                        one_ref[at] = flat - dual
                    else:
                        dual = refs[len(chunks)][at] + value - flat
                        one_ref[at] = flat
                    two_ref[at] = dual


def smooth(chunks, first, place, solved, sums, gains, extra, dims, token):
    operands = [solved, sums, *gains, *extra]
    shapes = [jax.ShapeDtypeStruct(dims, jnp.float32)] * 2
    kernel = functools.partial(smooth_kernel, chunks, first, dims[3])
    return run(kernel, token, [SCALARS] + [WHOLE] * len(operands), shapes, [place, *operands])


def assemble_kernel(chunks, sizes, line, share, place_ref, *refs):
    out_ref = refs[-1]
    refs = list(refs)
    for size, (t0, t1, f0, f1) in zip(sizes, chunks):
        blocks = [refs.pop(0) for _ in range(size)]
        for r in range(line):
            offset = pl.multiple_of((place_ref[0] ^ r) * share, LANES)
            out_ref[:, :, t0:t1, f0:f1, pl.ds(offset, share)] = block_of(blocks, r)


def assemble(chunks, line, place, gains, dims):
    share = dims[-1] // line
    if share % LANES:
        whole = jnp.zeros(dims, jnp.float32)
        for (t0, t1, f0, f1), blocks in zip(chunks, gains):
            stacked = jnp.stack([block_of(blocks, r) for r in range(line)])
            parts = [lax.dynamic_index_in_dim(stacked, place[0] ^ r, 0, False) for r in range(line)]
            whole = whole.at[:, :, t0:t1, f0:f1].set(jnp.concatenate(parts, axis=-1))
        return whole
    flat = [block for blocks in gains for block in blocks]
    kernel = functools.partial(assemble_kernel, chunks, [len(blocks) for blocks in gains], line, share)
    shapes = [jax.ShapeDtypeStruct(dims, jnp.float32)]
    return run(kernel, [], [SCALARS] + [WHOLE] * len(flat), shapes, [place, *flat])[0]


def shards(visibilities, coherencies, start_gains, penalty, stations):
    dims = start_gains.shape
    _, dirs, times, chans, count = dims
    line = lax.axis_size("bl")
    index = lax.axis_index("bl")
    place = jnp.stack([index, lax.axis_index("chan")]).astype(jnp.int32)
    groups = lax.axis_size("chan")
    share = count // line
    basis, solved = [jnp.asarray(table) for table in bernstein_tables(chans * groups)]

    def swap(values, axis, size, bit):
        return lax.ppermute(values, axis, [(i, i ^ bit) for i in range(size)])

    def chan_steps(values):
        steps = [values]
        bit = 1
        while bit < groups:
            steps.append(steps[-1] + swap(steps[-1], "chan", groups, bit))
            bit *= 2
        return steps

    ordered = start_gains
    if share % LANES:
        parts = [lax.dynamic_slice_in_dim(start_gains, (index ^ r) * share, share, 4) for r in range(line)]
        ordered = jnp.concatenate(parts, axis=4)
    own_dims = dims[:4] + (share,)
    chunks = chunks_of(times, chans)
    token = []
    gains = own = targets = duals = projected = None

    direct_order = list(range(1, line))
    zeros = jnp.zeros((times, POLY, 2, dirs, share), jnp.float32)
    for iteration in range(ITERS):
        first = iteration == 0
        parts, fresh = [], []
        if not first:
            picks = make_picks(line, count, place, stations, token)
            token = [picks]
        for c, chunk in enumerate(chunks):
            fill = first and c == 0
            source = [ordered] if first else gains[c]
            ends = stations if fill else picks
            out = normals(chunk, line, first, fill, place, source, visibilities, coherencies, ends, token)
            token = [out[0]]
            parts.append([out[0], swap(out[1], "bl", line, 1)])
            rest = list(out[2:])
            if first:
                fresh.append(rest.pop(0))
            if fill:
                picks, ordered, visibilities, coherencies = rest
        if first:
            own = fresh
        bit = 2
        while bit < line:
            for c in range(len(chunks)):
                waits = [steps[ADD_AFTER]] if ADD_AFTER and c and not first else []
                keep, send = add_parts(*parts[c], token + waits)
                parts[c] = [keep, swap(send, "bl", line, bit)]
                token = [keep]
            bit *= 2
        fresh, arrived = [], []
        projected = zeros
        for c, chunk in enumerate(chunks):
            extra = [own[c]] if first else [own[c], targets, duals]
            new, projected = update(chunk, first, chans, penalty, place, basis, projected, parts[c], extra, token)
            token = [new]
            fresh.append(new)
            direct = not first and c == len(chunks) - 1
            arrived.append([swap(new[None], "bl", line, r) for r in (direct_order if direct else [line // 2])])
        own = fresh
        steps = chan_steps(projected)
        gains = []
        for c in range(len(chunks)):
            blocks, got, bit = own[c][None], arrived[c][0], line // 2
            if len(arrived[c]) > 1:
                gains.append([blocks] + [arrived[c][direct_order.index(r)] for r in range(1, line)])
                continue
            after = JOIN_AFTER[iteration][min(c, 1)]
            while bit > 1:
                if after:
                    blocks = join(blocks, got, [steps[after]])
                else:
                    blocks = jnp.stack([blocks, got], axis=1).reshape((2 * blocks.shape[0],) + blocks.shape[1:])
                bit //= 2
                got = swap(blocks, "bl", line, bit)
            gains.append([blocks, got])
        if first:
            targets, duals = smooth(chunks, True, place, solved, steps[-1], own, [], own_dims, [])
    consensus, dual = smooth(chunks, False, place, solved, steps[-1], own, [duals], own_dims, [])
    return assemble(chunks, line, place, gains, dims), consensus, dual


def solution(mesh):
    in_specs = (
        P(None, None, "chan", "bl"),
        P(None, None, None, "chan", "bl"),
        P(None, None, None, "chan", None),
        P(),
        P(None, "bl"),
    )
    out_specs = (
        P(None, None, None, "chan", None),
        P(None, None, None, "chan", "bl"),
        P(None, None, None, "chan", "bl"),
    )
    return jax.shard_map(shards, mesh=mesh, in_specs=in_specs, out_specs=out_specs, check_vma=False)
```

```python
import functools
import math

import jax
import jax.numpy as jnp
import numpy as np
from jax import lax
from jax.experimental import pallas as pl
from jax.experimental.pallas import tpu as pltpu
from jax.sharding import PartitionSpec as P

POLY = 4
ITERS = 2
LANES = 128
SUBLANES = 8
JOIN_AFTER = ((0, 0), (1, 2))
ADD_AFTER = 2
ROWS_BY_COLS = (((1,), (0,)), ((), ()))
ROWS_BY_ROWS = (((1,), (1,)), ((), ()))
VMEM = pltpu.MemorySpace.VMEM
HBM = pltpu.MemorySpace.HBM
WHOLE = pl.BlockSpec(memory_space=VMEM)
OUTSIDE = pl.BlockSpec(memory_space=pl.ANY)
CHEAP = pl.CostEstimate(flops=2**20, bytes_accessed=2**10, transcendentals=0)


def run(kernel, token, in_specs, out_shape, operands, scratch=(), limit=4):
    count = len(token)
    return pl.pallas_call(
        lambda *refs: kernel(*refs[count:]),
        in_specs=[OUTSIDE] * count + list(in_specs),
        out_specs=[WHOLE] * len(out_shape),
        out_shape=list(out_shape),
        scratch_shapes=list(scratch),
        compiler_params=pltpu.CompilerParams(vmem_limit_bytes=limit * 2**20),
        cost_estimate=CHEAP,
    )(*token, *operands)


def bernstein_tables(total):
    position = (np.arange(total) + 0.5) / total
    basis = np.stack(
        [math.comb(POLY - 1, j) * position**j * (1.0 - position) ** (POLY - 1 - j) for j in range(POLY)], axis=1
    )
    factor = np.linalg.cholesky(basis.T @ basis)
    solved = np.linalg.solve(factor.T, np.linalg.solve(factor, basis.T)).T
    return basis.astype(np.float32), solved.astype(np.float32)


def split(values):
    upper = values.astype(jnp.bfloat16)
    return upper, (values - upper.astype(jnp.float32)).astype(jnp.bfloat16)


def chunks_of(times, chans):
    return [(t, t + 1, 0, chans) for t in range(times)]


def block_of(refs, r):
    return refs[r % 2][r // 2] if len(refs) == 2 else refs[r][0]


def normals_kernel(chunk, line, share, start, fill, sources, *refs):
    t0, t1, f0, f1 = chunk
    refs = list(refs)
    gain_refs = [refs.pop(0) for _ in range(sources)]
    vis_ref, coh_ref, pick_ref = [refs.pop(0) for _ in range(3)]
    outs = [refs.pop(0) for _ in range(2)]
    own_ref = refs.pop(0) if start else None
    dirs, links = coh_ref.shape[1], coh_ref.shape[4]
    rows = (t1 - t0) * (f1 - f0)
    copies = []
    if fill:
        offsets = block_offsets(line, share)
        moves = [(r * share, share, pl.multiple_of(offsets[r], LANES)) for r in range(line)]
        if share % LANES:
            moves = [(0, line * share, 0)]
        station_hbm, pick_ref = pick_ref, refs.pop(0)
        station_ref, sems = refs[-2:]
        pairs = [(station_hbm, station_ref)]
        for t in range(vis_ref.shape[1]):
            for to, size, at in moves:
                gain_from = gain_refs[0].at[:, :, t, :, pl.ds(at, size)]
                pairs.append((gain_from, refs[0].at[:, :, t, :, pl.ds(to, size)]))
            pairs += [(vis_ref.at[:, t], refs[1].at[:, t]), (coh_ref.at[:, :, t], refs[2].at[:, :, t])]
        each = len(moves) + 2
        gain_refs, vis_ref, coh_ref = [refs[0]], refs[1], refs[2]
        copies = [pltpu.make_async_copy(src, dst, sems.at[i]) for i, (src, dst) in enumerate(pairs)]
        for copy in copies:
            copy.start()
        copies[0].wait()
        for t in range(t0, t1):
            for copy in copies[1 + each * t : each * t + each - 1]:
                copy.wait()
        build_picks(line, share, offsets, station_ref, pick_ref)
    if start:
        blocks = [gain_refs[0][:, :, t0:t1, f0:f1, r * share : (r + 1) * share] for r in range(line)]
        own_ref[...] = blocks[0]
    else:
        blocks = [block_of(gain_refs, r) for r in range(line)]
    blocks = [block.reshape(2 * dirs * rows, share) for block in blocks]
    dot = functools.partial(lax.dot_general, preferred_element_type=jnp.float32)
    both = jnp.concatenate(split(jnp.concatenate(blocks, axis=1)), axis=0)
    wide = [dot(both, pick_ref[end], ROWS_BY_COLS) for end in range(2)]
    height = 2 * dirs * rows
    first, second = [values[:height] + values[height:] for values in wide]

    def row(values, part, k):
        begin = (part * dirs + k) * rows
        return values[begin : begin + rows]

    def coherency(part, k):
        low = f0 // 16 * 16
        high = min(-(-f1 // 16) * 16, coh_ref.shape[3])
        values = coh_ref[part, k, t0:t1, low:high].astype(jnp.float32)
        return values[:, f0 - low : f1 - low].reshape(rows, links)

    for t in range(t0, t1 if fill else t0):
        copies[each * t + each - 1].wait()
        copies[each * t + each].wait()
    rest_real = vis_ref[0, t0:t1, f0:f1].reshape(rows, links)
    rest_imag = vis_ref[1, t0:t1, f0:f1].reshape(rows, links)
    sides = []
    for k in range(dirs):
        coh_real, coh_imag = coherency(0, k), coherency(1, k)
        first_real, first_imag = row(first, 0, k), row(first, 1, k)
        second_real, second_imag = row(second, 0, k), row(second, 1, k)
        left_real = second_real * coh_real + second_imag * coh_imag
        left_imag = second_imag * coh_real - second_real * coh_imag
        right_real = first_real * coh_real - first_imag * coh_imag
        right_imag = first_real * coh_imag + first_imag * coh_real
        rest_real = rest_real - (first_real * left_real + first_imag * left_imag)
        rest_imag = rest_imag - (first_imag * left_real - first_real * left_imag)
        sides.append((left_real, left_imag, right_real, right_imag))
    terms = [[], []]
    terms[0] += [rest_real * a - rest_imag * b for a, b, _, _ in sides]
    terms[0] += [rest_real * b + rest_imag * a for a, b, _, _ in sides]
    terms[0] += [a * a + b * b for a, b, _, _ in sides]
    terms[1] += [rest_real * c + rest_imag * d for _, _, c, d in sides]
    terms[1] += [rest_real * d - rest_imag * c for _, _, c, d in sides]
    terms[1] += [c * c + d * d for _, _, c, d in sides]
    pieces = [split(jnp.concatenate(terms[end], axis=0)) for end in range(2)]
    wide = jnp.concatenate([pick_ref[0], pick_ref[1]], axis=1)
    total = None
    for part in range(2):
        value = dot(jnp.concatenate([pieces[0][part], pieces[1][part]], axis=1), wide, ROWS_BY_ROWS)
        total = value if total is None else total + value
    for r in range(line):
        piece = total[:, r * share : (r + 1) * share].reshape(3, dirs, t1 - t0, f1 - f0, share)
        outs[r % 2][r // 2] = piece
    for t in range(vis_ref.shape[1] if fill else 0):
        if not t0 <= t < t1:
            for copy in copies[1 + each * t : 1 + each * t + each]:
                copy.wait()


def block_offsets(line, share):
    place = lax.axis_index("bl")
    return [(place ^ r) * share for r in range(line)]


def build_picks(line, share, offsets, station_ref, pick_ref):
    links = station_ref.shape[1]
    one, zero = jnp.ones((), jnp.bfloat16), jnp.zeros((), jnp.bfloat16)
    ids = lax.broadcasted_iota(jnp.int32, (share, links), 0).astype(jnp.float32).astype(jnp.bfloat16)
    for end in range(2):
        for r in range(line):
            number = station_ref[end : end + 1, :] - offsets[r]
            number = jnp.where((number >= 0) & (number < share), number, -1)
            number = number.astype(jnp.float32).astype(jnp.bfloat16)
            pick_ref[end, r * share : (r + 1) * share] = jnp.where(ids == number, one, zero)


def picks_kernel(line, share, station_ref, pick_ref):
    build_picks(line, share, block_offsets(line, share), station_ref, pick_ref)


def make_picks(line, count, stations, token):
    shapes = [VMEM((2, count, stations.shape[1]), jnp.bfloat16)]
    kernel = functools.partial(picks_kernel, line, count // line)
    return run(kernel, token, [WHOLE], shapes, [stations], (), 8)[0]


def normals(chunk, line, start, fill, gains, visibilities, coherencies, picks, token):
    t0, t1, f0, f1 = chunk
    dirs, links = coherencies.shape[1], coherencies.shape[4]
    count = gains[0].shape[-1] if start else gains[0].shape[-1] * line
    share = count // line
    piece = (dirs, t1 - t0, f1 - f0, share)
    shapes = [jax.ShapeDtypeStruct((line // 2, 3) + piece, jnp.float32)] * 2
    scratch = []
    if start:
        shapes.append(jax.ShapeDtypeStruct((2,) + piece, jnp.float32))
    if fill:
        shapes.append(VMEM((2, count, links), jnp.bfloat16))
        times = visibilities.shape[1]
        scratch = [pltpu.VMEM((2, links), jnp.int32), pltpu.SemaphoreType.DMA((1 + (line + 2) * times,))]
        shapes += [VMEM(x.shape, x.dtype) for x in (gains[0], visibilities, coherencies)]
    spaces = [HBM if fill else VMEM] * (len(gains) + 3)
    sources = [*gains, visibilities, coherencies, picks]
    sources = [pltpu.with_memory_space_constraint(x, space) for x, space in zip(sources, spaces)]
    specs = [OUTSIDE if space is HBM else WHOLE for space in spaces]
    kernel = functools.partial(normals_kernel, chunk, line, share, start, fill, len(gains))
    return run(kernel, token, specs, shapes, sources, scratch, 32)


def add_kernel(keep_ref, got_ref, own_ref, send_ref):
    for i in range(own_ref.shape[0]):
        own_ref[i] = keep_ref[2 * i] + got_ref[2 * i]
        send_ref[i] = keep_ref[2 * i + 1] + got_ref[2 * i + 1]


def add_parts(keep, got, token):
    shape = jax.ShapeDtypeStruct((keep.shape[0] // 2,) + keep.shape[1:], keep.dtype)
    return run(add_kernel, token, [WHOLE] * 2, [shape] * 2, [keep, got])


def join_kernel(blocks_ref, got_ref, out_ref):
    for i in range(blocks_ref.shape[0]):
        out_ref[2 * i] = blocks_ref[i]
        out_ref[2 * i + 1] = got_ref[i]


def join(blocks, got, token):
    shape = jax.ShapeDtypeStruct((2 * blocks.shape[0],) + blocks.shape[1:], blocks.dtype)
    return run(join_kernel, token, [WHOLE] * 2, [shape], [blocks, got])[0]


def update_kernel(chunk, parts, first, penalty_ref, table_ref, before_ref, *refs):
    t0, t1, f0, f1 = chunk
    part_refs = refs[:parts]
    extra = refs[parts:-2]
    new_ref, sum_ref = refs[-2:]
    sum_ref[...] = before_ref[...]
    basis = table_ref[f0:f1]
    for k in range(new_ref.shape[1]):
        load = penalty_ref[k : k + 1]
        for t in range(t0, t1):
            weight = sum(ref[0, 2, k, t - t0] for ref in part_refs)
            divisor = weight + load
            for part in range(2):
                gain = extra[0][part, k, t - t0]
                target = gain if first else extra[1][part, k, t, f0:f1]
                total = sum(ref[0, part, k, t - t0] for ref in part_refs)
                new = (total + gain * weight + load * target) / divisor
                new_ref[part, k, t - t0] = new
                value = new if first else new + extra[2][part, k, t, f0:f1]
                for j in range(POLY):
                    row = jnp.sum(basis[:, j : j + 1] * value, axis=0, keepdims=True)
                    sum_ref[t, j, part, k : k + 1] += row


def update(chunk, first, penalty, table, before, parts, extra, token):
    shapes = [
        jax.ShapeDtypeStruct((2,) + parts[0].shape[2:], jnp.float32),
        jax.ShapeDtypeStruct(before.shape, jnp.float32),
    ]
    operands = [penalty, table, before, *parts, *extra]
    kernel = functools.partial(update_kernel, chunk, len(parts), first)
    return run(kernel, token, [WHOLE] * len(operands), shapes, operands)


def smooth_kernel(chunks, first, table_ref, sum_ref, *refs):
    one_ref, two_ref = refs[-2:]
    solved = table_ref[:, POLY:]
    for (t0, t1, f0, f1), gain_ref in zip(chunks, refs):
        for part in range(2):
            for k in range(one_ref.shape[1]):
                for t in range(t0, t1):
                    flat = sum(
                        solved[f0:f1, j : j + 1] * sum_ref[t, j, part, k : k + 1] for j in range(POLY)
                    )
                    value = gain_ref[part, k, t - t0]
                    at = (part, k, t, slice(f0, f1))
                    if first:
                        dual = value - flat
                        one_ref[at] = flat - dual
                    else:
                        dual = refs[len(chunks)][at] + value - flat
                        one_ref[at] = flat
                    two_ref[at] = dual


def smooth(chunks, first, table, sums, gains, extra, dims, token):
    operands = [table, sums, *gains, *extra]
    shapes = [jax.ShapeDtypeStruct(dims, jnp.float32)] * 2
    kernel = functools.partial(smooth_kernel, chunks, first)
    return run(kernel, token, [WHOLE] * len(operands), shapes, operands)


def assemble_kernel(chunks, sizes, line, share, *refs):
    out_ref = refs[-1]
    refs = list(refs)
    offsets = block_offsets(line, share)
    for size, (t0, t1, f0, f1) in zip(sizes, chunks):
        blocks = [refs.pop(0) for _ in range(size)]
        for r in range(line):
            offset = pl.multiple_of(offsets[r], LANES)
            out_ref[:, :, t0:t1, f0:f1, pl.ds(offset, share)] = block_of(blocks, r)


def assemble(chunks, line, place, gains, dims):
    share = dims[-1] // line
    if share % LANES:
        whole = jnp.zeros(dims, jnp.float32)
        for (t0, t1, f0, f1), blocks in zip(chunks, gains):
            stacked = jnp.stack([block_of(blocks, r) for r in range(line)])
            parts = [lax.dynamic_index_in_dim(stacked, place ^ r, 0, False) for r in range(line)]
            whole = whole.at[:, :, t0:t1, f0:f1].set(jnp.concatenate(parts, axis=-1))
        return whole
    flat = [block for blocks in gains for block in blocks]
    kernel = functools.partial(assemble_kernel, chunks, [len(blocks) for blocks in gains], line, share)
    shapes = [jax.ShapeDtypeStruct(dims, jnp.float32)]
    return run(kernel, [], [WHOLE] * len(flat), shapes, flat)[0]


def shards(visibilities, coherencies, start_gains, penalty, stations):
    dims = start_gains.shape
    _, dirs, times, chans, count = dims
    line = lax.axis_size("bl")
    index = lax.axis_index("bl")
    groups = lax.axis_size("chan")
    share = count // line
    tables = jnp.asarray(np.concatenate(bernstein_tables(chans * groups), axis=1))
    table = lax.dynamic_slice_in_dim(tables, lax.axis_index("chan") * chans, chans, 0)
    loads = jnp.broadcast_to(penalty[:, None], (dirs, share))

    def swap(values, axis, size, bit):
        return lax.ppermute(values, axis, [(i, i ^ bit) for i in range(size)])

    def chan_steps(values):
        steps = [values]
        bit = 1
        while bit < groups:
            steps.append(steps[-1] + swap(steps[-1], "chan", groups, bit))
            bit *= 2
        return steps

    ordered = start_gains
    if share % LANES:
        parts = [lax.dynamic_slice_in_dim(start_gains, (index ^ r) * share, share, 4) for r in range(line)]
        ordered = jnp.concatenate(parts, axis=4)
    own_dims = dims[:4] + (share,)
    chunks = chunks_of(times, chans)
    token = []
    gains = own = targets = duals = projected = None

    direct_order = list(range(1, line))
    zeros = jnp.zeros((times, POLY, 2, dirs, share), jnp.float32)
    for iteration in range(ITERS):
        first = iteration == 0
        parts, fresh = [], []
        if not first:
            picks = make_picks(line, count, stations, token)
            token = [picks]
        for c, chunk in enumerate(chunks):
            fill = first and c == 0
            source = [ordered] if first else gains[c]
            ends = stations if fill else picks
            out = normals(chunk, line, first, fill, source, visibilities, coherencies, ends, token)
            token = [out[0]]
            parts.append([out[0], swap(out[1], "bl", line, 1)])
            rest = list(out[2:])
            if first:
                fresh.append(rest.pop(0))
            if fill:
                picks, ordered, visibilities, coherencies = rest
        if first:
            own = fresh
        bit = 2
        while bit < line:
            for c in range(len(chunks)):
                waits = [steps[ADD_AFTER]] if ADD_AFTER and c and not first else []
                keep, send = add_parts(*parts[c], token + waits)
                parts[c] = [keep, swap(send, "bl", line, bit)]
                token = [keep]
            bit *= 2
        fresh, arrived = [], []
        projected = zeros
        for c, chunk in enumerate(chunks):
            extra = [own[c]] if first else [own[c], targets, duals]
            new, projected = update(chunk, first, loads, table, projected, parts[c], extra, token)
            token = [new]
            fresh.append(new)
            direct = not first and c == len(chunks) - 1
            arrived.append([swap(new[None], "bl", line, r) for r in (direct_order if direct else [line // 2])])
        own = fresh
        steps = chan_steps(projected)
        gains = []
        for c in range(len(chunks)):
            blocks, got, bit = own[c][None], arrived[c][0], line // 2
            if len(arrived[c]) > 1:
                gains.append([blocks] + [arrived[c][direct_order.index(r)] for r in range(1, line)])
                continue
            after = JOIN_AFTER[iteration][min(c, 1)]
            while bit > 1:
                if after:
                    blocks = join(blocks, got, [steps[after]])
                else:
                    blocks = jnp.stack([blocks, got], axis=1).reshape((2 * blocks.shape[0],) + blocks.shape[1:])
                bit //= 2
                got = swap(blocks, "bl", line, bit)
            gains.append([blocks, got])
        if first:
            targets, duals = smooth(chunks, True, table, steps[-1], own, [], own_dims, [])
    consensus, dual = smooth(chunks, False, table, steps[-1], own, [duals], own_dims, [])
    return assemble(chunks, line, index, gains, dims), consensus, dual


def solution(mesh):
    in_specs = (
        P(None, None, "chan", "bl"),
        P(None, None, None, "chan", "bl"),
        P(None, None, None, "chan", None),
        P(),
        P(None, "bl"),
    )
    out_specs = (
        P(None, None, None, "chan", None),
        P(None, None, None, "chan", "bl"),
        P(None, None, None, "chan", "bl"),
    )
    return jax.shard_map(shards, mesh=mesh, in_specs=in_specs, out_specs=out_specs, check_vma=False)
```

```python
import functools
import math

import jax
import jax.numpy as jnp
import numpy as np
from jax import lax
from jax.experimental import pallas as pl
from jax.experimental.pallas import tpu as pltpu
from jax.sharding import PartitionSpec as P

POLY = 4
ITERS = 2
LANES = 128
SUBLANES = 8
JOIN_AFTER = ((0, 0), (1, 2))
ADD_AFTER = 2
ROWS_BY_COLS = (((1,), (0,)), ((), ()))
ROWS_BY_ROWS = (((1,), (1,)), ((), ()))
VMEM = pltpu.MemorySpace.VMEM
HBM = pltpu.MemorySpace.HBM
WHOLE = pl.BlockSpec(memory_space=VMEM)
OUTSIDE = pl.BlockSpec(memory_space=pl.ANY)
CHEAP = pl.CostEstimate(flops=2**20, bytes_accessed=2**10, transcendentals=0)


def run(kernel, token, in_specs, out_shape, operands, scratch=(), limit=4):
    count = len(token)
    return pl.pallas_call(
        lambda *refs: kernel(*refs[count:]),
        in_specs=[OUTSIDE] * count + list(in_specs),
        out_specs=[WHOLE] * len(out_shape),
        out_shape=list(out_shape),
        scratch_shapes=list(scratch),
        compiler_params=pltpu.CompilerParams(vmem_limit_bytes=limit * 2**20),
        cost_estimate=CHEAP,
    )(*token, *operands)


def bernstein_tables(total):
    position = (np.arange(total) + 0.5) / total
    basis = np.stack(
        [math.comb(POLY - 1, j) * position**j * (1.0 - position) ** (POLY - 1 - j) for j in range(POLY)], axis=1
    )
    factor = np.linalg.cholesky(basis.T @ basis)
    solved = np.linalg.solve(factor.T, np.linalg.solve(factor, basis.T)).T
    return basis.astype(np.float32), solved.astype(np.float32)


def split(values):
    upper = values.astype(jnp.bfloat16)
    return upper, (values - upper.astype(jnp.float32)).astype(jnp.bfloat16)


def chunks_of(times, chans):
    return [(t, t + 1, 0, chans) for t in range(times)]


def block_of(refs, r):
    return refs[r % 2][r // 2] if len(refs) == 2 else refs[r][0]


def normals_kernel(chunk, line, share, start, fill, sources, *refs):
    t0, t1, f0, f1 = chunk
    refs = list(refs)
    gain_refs = [refs.pop(0) for _ in range(sources)]
    vis_ref, coh_ref, pick_ref = [refs.pop(0) for _ in range(3)]
    outs = [refs.pop(0) for _ in range(2)]
    own_ref = refs.pop(0) if start else None
    dirs, links = coh_ref.shape[1], coh_ref.shape[4]
    rows = (t1 - t0) * (f1 - f0)
    copies = []
    if fill:
        offsets = block_offsets(line, share)
        moves = [(r * share, share, pl.multiple_of(offsets[r], LANES)) for r in range(line)]
        if share % LANES:
            moves = [(0, line * share, 0)]
        station_hbm, pick_ref = pick_ref, refs.pop(0)
        station_ref, sems = refs[-2:]
        pairs = [(station_hbm, station_ref)]
        for t in range(vis_ref.shape[1]):
            for to, size, at in moves:
                gain_from = gain_refs[0].at[:, :, t, :, pl.ds(at, size)]
                pairs.append((gain_from, refs[0].at[:, :, t, :, pl.ds(to, size)]))
            pairs += [(vis_ref.at[:, t], refs[1].at[:, t]), (coh_ref.at[:, :, t], refs[2].at[:, :, t])]
        each = len(moves) + 2
        gain_refs, vis_ref, coh_ref = [refs[0]], refs[1], refs[2]
        copies = [pltpu.make_async_copy(src, dst, sems.at[i]) for i, (src, dst) in enumerate(pairs)]
        for copy in copies:
            copy.start()
        copies[0].wait()
        for t in range(t0, t1):
            for copy in copies[1 + each * t : each * t + each - 1]:
                copy.wait()
        build_picks(line, share, offsets, station_ref, pick_ref)
    if start:
        blocks = [gain_refs[0][:, :, t0:t1, f0:f1, r * share : (r + 1) * share] for r in range(line)]
        own_ref[...] = blocks[0]
    else:
        blocks = [block_of(gain_refs, r) for r in range(line)]
    blocks = [block.reshape(2 * dirs * rows, share) for block in blocks]
    dot = functools.partial(lax.dot_general, preferred_element_type=jnp.float32)
    both = jnp.concatenate(split(jnp.concatenate(blocks, axis=1)), axis=0)
    wide = [dot(both, pick_ref[end], ROWS_BY_COLS) for end in range(2)]
    height = 2 * dirs * rows
    first, second = [values[:height] + values[height:] for values in wide]

    def row(values, part, k):
        begin = (part * dirs + k) * rows
        return values[begin : begin + rows]

    def coherency(part, k):
        low = f0 // 16 * 16
        high = min(-(-f1 // 16) * 16, coh_ref.shape[3])
        values = coh_ref[part, k, t0:t1, low:high].astype(jnp.float32)
        return values[:, f0 - low : f1 - low].reshape(rows, links)

    for t in range(t0, t1 if fill else t0):
        copies[each * t + each - 1].wait()
        copies[each * t + each].wait()
    rest_real = vis_ref[0, t0:t1, f0:f1].reshape(rows, links)
    rest_imag = vis_ref[1, t0:t1, f0:f1].reshape(rows, links)
    sides = []
    for k in range(dirs):
        coh_real, coh_imag = coherency(0, k), coherency(1, k)
        first_real, first_imag = row(first, 0, k), row(first, 1, k)
        second_real, second_imag = row(second, 0, k), row(second, 1, k)
        left_real = second_real * coh_real + second_imag * coh_imag
        left_imag = second_imag * coh_real - second_real * coh_imag
        right_real = first_real * coh_real - first_imag * coh_imag
        right_imag = first_real * coh_imag + first_imag * coh_real
        rest_real = rest_real - (first_real * left_real + first_imag * left_imag)
        rest_imag = rest_imag - (first_imag * left_real - first_real * left_imag)
        sides.append((left_real, left_imag, right_real, right_imag))
    terms = [[], []]
    terms[0] += [rest_real * a - rest_imag * b for a, b, _, _ in sides]
    terms[0] += [rest_real * b + rest_imag * a for a, b, _, _ in sides]
    terms[0] += [a * a + b * b for a, b, _, _ in sides]
    terms[1] += [rest_real * c + rest_imag * d for _, _, c, d in sides]
    terms[1] += [rest_real * d - rest_imag * c for _, _, c, d in sides]
    terms[1] += [c * c + d * d for _, _, c, d in sides]
    pieces = [split(jnp.concatenate(terms[end], axis=0)) for end in range(2)]
    wide = jnp.concatenate([pick_ref[0], pick_ref[1]], axis=1)
    total = None
    for part in range(2):
        value = dot(jnp.concatenate([pieces[0][part], pieces[1][part]], axis=1), wide, ROWS_BY_ROWS)
        total = value if total is None else total + value
    for r in range(line):
        piece = total[:, r * share : (r + 1) * share].reshape(3, dirs, t1 - t0, f1 - f0, share)
        outs[r % 2][r // 2] = piece
    for t in range(vis_ref.shape[1] if fill else 0):
        if not t0 <= t < t1:
            for copy in copies[1 + each * t : 1 + each * t + each]:
                copy.wait()


def block_offsets(line, share):
    place = lax.axis_index("bl")
    return [(place ^ r) * share for r in range(line)]


def build_picks(line, share, offsets, station_ref, pick_ref):
    links = station_ref.shape[1]
    one, zero = jnp.ones((), jnp.bfloat16), jnp.zeros((), jnp.bfloat16)
    ids = lax.broadcasted_iota(jnp.int32, (share, links), 0).astype(jnp.float32).astype(jnp.bfloat16)
    for end in range(2):
        for r in range(line):
            number = station_ref[end : end + 1, :] - offsets[r]
            number = jnp.where((number >= 0) & (number < share), number, -1)
            number = number.astype(jnp.float32).astype(jnp.bfloat16)
            pick_ref[end, r * share : (r + 1) * share] = jnp.where(ids == number, one, zero)


def picks_kernel(line, share, station_ref, pick_ref):
    build_picks(line, share, block_offsets(line, share), station_ref, pick_ref)


def make_picks(line, count, stations, token):
    shapes = [VMEM((2, count, stations.shape[1]), jnp.bfloat16)]
    kernel = functools.partial(picks_kernel, line, count // line)
    return run(kernel, token, [WHOLE], shapes, [stations], (), 8)[0]


def normals(chunk, line, start, fill, gains, visibilities, coherencies, picks, token):
    t0, t1, f0, f1 = chunk
    dirs, links = coherencies.shape[1], coherencies.shape[4]
    count = gains[0].shape[-1] if start else gains[0].shape[-1] * line
    share = count // line
    piece = (dirs, t1 - t0, f1 - f0, share)
    shapes = [jax.ShapeDtypeStruct((line // 2, 3) + piece, jnp.float32)] * 2
    scratch = []
    if start:
        shapes.append(jax.ShapeDtypeStruct((2,) + piece, jnp.float32))
    if fill:
        shapes.append(VMEM((2, count, links), jnp.bfloat16))
        times = visibilities.shape[1]
        scratch = [pltpu.VMEM((2, links), jnp.int32), pltpu.SemaphoreType.DMA((1 + (line + 2) * times,))]
        shapes += [VMEM(x.shape, x.dtype) for x in (gains[0], visibilities, coherencies)]
    spaces = [HBM if fill else VMEM] * (len(gains) + 3)
    sources = [*gains, visibilities, coherencies, picks]
    sources = [pltpu.with_memory_space_constraint(x, space) for x, space in zip(sources, spaces)]
    specs = [OUTSIDE if space is HBM else WHOLE for space in spaces]
    kernel = functools.partial(normals_kernel, chunk, line, share, start, fill, len(gains))
    return run(kernel, token, specs, shapes, sources, scratch, 32)


def add_kernel(keep_ref, got_ref, own_ref, send_ref):
    for i in range(own_ref.shape[0]):
        own_ref[i] = keep_ref[2 * i] + got_ref[2 * i]
        send_ref[i] = keep_ref[2 * i + 1] + got_ref[2 * i + 1]


def add_parts(keep, got, token):
    shape = jax.ShapeDtypeStruct((keep.shape[0] // 2,) + keep.shape[1:], keep.dtype)
    return run(add_kernel, token, [WHOLE] * 2, [shape] * 2, [keep, got])


def join_kernel(blocks_ref, got_ref, out_ref):
    for i in range(blocks_ref.shape[0]):
        out_ref[2 * i] = blocks_ref[i]
        out_ref[2 * i + 1] = got_ref[i]


def join(blocks, got, token):
    shape = jax.ShapeDtypeStruct((2 * blocks.shape[0],) + blocks.shape[1:], blocks.dtype)
    return run(join_kernel, token, [WHOLE] * 2, [shape], [blocks, got])[0]


def update_kernel(chunk, parts, first, penalty_ref, table_ref, before_ref, *refs):
    t0, t1, f0, f1 = chunk
    part_refs = refs[:parts]
    extra = refs[parts:-2]
    new_ref, sum_ref = refs[-2:]
    sum_ref[...] = before_ref[...]
    basis = table_ref[f0:f1]
    for k in range(new_ref.shape[1]):
        load = penalty_ref[k : k + 1]
        for t in range(t0, t1):
            weight = sum(ref[0, 2, k, t - t0] for ref in part_refs)
            divisor = weight + load
            for part in range(2):
                gain = extra[0][part, k, t - t0]
                target = gain if first else extra[1][part, k, t, f0:f1]
                total = sum(ref[0, part, k, t - t0] for ref in part_refs)
                new = (total + gain * weight + load * target) / divisor
                new_ref[part, k, t - t0] = new
                value = new if first else new + extra[2][part, k, t, f0:f1]
                for j in range(POLY):
                    row = jnp.sum(basis[:, j : j + 1] * value, axis=0, keepdims=True)
                    sum_ref[t, j, part, k : k + 1] += row


def update(chunk, first, penalty, table, before, parts, extra, token):
    shapes = [
        jax.ShapeDtypeStruct((2,) + parts[0].shape[2:], jnp.float32),
        jax.ShapeDtypeStruct(before.shape, jnp.float32),
    ]
    operands = [penalty, table, before, *parts, *extra]
    kernel = functools.partial(update_kernel, chunk, len(parts), first)
    return run(kernel, token, [WHOLE] * len(operands), shapes, operands)


def smooth_kernel(chunks, first, table_ref, sum_ref, *refs):
    one_ref, two_ref = refs[-2:]
    solved = table_ref[:, POLY:]
    for (t0, t1, f0, f1), gain_ref in zip(chunks, refs):
        for part in range(2):
            for k in range(one_ref.shape[1]):
                for t in range(t0, t1):
                    flat = sum(
                        solved[f0:f1, j : j + 1] * sum_ref[t, j, part, k : k + 1] for j in range(POLY)
                    )
                    value = gain_ref[part, k, t - t0]
                    at = (part, k, t, slice(f0, f1))
                    if first:
                        dual = value - flat
                        one_ref[at] = flat - dual
                    else:
                        dual = refs[len(chunks)][at] + value - flat
                        one_ref[at] = flat
                    two_ref[at] = dual


def smooth(chunks, first, table, sums, gains, extra, dims, token):
    operands = [table, sums, *gains, *extra]
    shapes = [jax.ShapeDtypeStruct(dims, jnp.float32)] * 2
    kernel = functools.partial(smooth_kernel, chunks, first)
    return run(kernel, token, [WHOLE] * len(operands), shapes, operands)


def assemble_kernel(chunks, sizes, line, share, *refs):
    out_ref = refs[-1]
    refs = list(refs)
    offsets = block_offsets(line, share)
    for size, (t0, t1, f0, f1) in zip(sizes, chunks):
        blocks = [refs.pop(0) for _ in range(size)]
        for r in range(line):
            offset = pl.multiple_of(offsets[r], LANES)
            out_ref[:, :, t0:t1, f0:f1, pl.ds(offset, share)] = block_of(blocks, r)


def assemble(chunks, line, place, gains, dims):
    share = dims[-1] // line
    if share % LANES:
        whole = jnp.zeros(dims, jnp.float32)
        for (t0, t1, f0, f1), blocks in zip(chunks, gains):
            stacked = jnp.stack([block_of(blocks, r) for r in range(line)])
            parts = [lax.dynamic_index_in_dim(stacked, place ^ r, 0, False) for r in range(line)]
            whole = whole.at[:, :, t0:t1, f0:f1].set(jnp.concatenate(parts, axis=-1))
        return whole
    flat = [block for blocks in gains for block in blocks]
    kernel = functools.partial(assemble_kernel, chunks, [len(blocks) for blocks in gains], line, share)
    shapes = [jax.ShapeDtypeStruct(dims, jnp.float32)]
    return run(kernel, [], [WHOLE] * len(flat), shapes, flat)[0]


def shards(visibilities, coherencies, start_gains, penalty, stations):
    dims = start_gains.shape
    _, dirs, times, chans, count = dims
    line = lax.axis_size("bl")
    index = lax.axis_index("bl")
    groups = lax.axis_size("chan")
    share = count // line
    tables = jnp.asarray(np.concatenate(bernstein_tables(chans * groups), axis=1))
    table = lax.dynamic_slice_in_dim(tables, lax.axis_index("chan") * chans, chans, 0)
    loads = jnp.broadcast_to(penalty[:, None], (dirs, share))

    def swap(values, axis, size, bit):
        return lax.ppermute(values, axis, [(i, i ^ bit) for i in range(size)])

    def chan_steps(values):
        steps = [values]
        bit = 1
        while bit < groups:
            steps.append(steps[-1] + swap(steps[-1], "chan", groups, bit))
            bit *= 2
        return steps

    ordered = start_gains
    if share % LANES:
        parts = [lax.dynamic_slice_in_dim(start_gains, (index ^ r) * share, share, 4) for r in range(line)]
        ordered = jnp.concatenate(parts, axis=4)
    own_dims = dims[:4] + (share,)
    chunks = chunks_of(times, chans)
    token = []
    gains = own = targets = duals = projected = None

    direct_order = list(range(1, line))
    zeros = jnp.zeros((times, POLY, 2, dirs, share), jnp.float32)
    for iteration in range(ITERS):
        first = iteration == 0
        parts, fresh = [], []
        if not first:
            picks = make_picks(line, count, stations, token)
            token = [picks]
        for c, chunk in enumerate(chunks):
            fill = first and c == 0
            source = [ordered] if first else gains[c]
            ends = stations if fill else picks
            out = normals(chunk, line, first, fill, source, visibilities, coherencies, ends, token)
            token = [out[0]]
            parts.append([out[0], swap(out[1], "bl", line, 1)])
            rest = list(out[2:])
            if first:
                fresh.append(rest.pop(0))
            if fill:
                picks, ordered, visibilities, coherencies = rest
        if first:
            own = fresh
        bit = 2
        while bit < line:
            for c in range(len(chunks)):
                waits = [steps[ADD_AFTER]] if ADD_AFTER and c and not first else []
                keep, send = add_parts(*parts[c], token + waits)
                parts[c] = [keep, swap(send, "bl", line, bit)]
                token = [keep]
            bit *= 2
        fresh, arrived = [], []
        projected = zeros
        for c, chunk in enumerate(chunks):
            extra = [own[c]] if first else [own[c], targets, duals]
            new, projected = update(chunk, first, loads, table, projected, parts[c], extra, token)
            token = [new]
            fresh.append(new)
            direct = c == len(chunks) - 1
            arrived.append([swap(new[None], "bl", line, r) for r in (direct_order if direct else [line // 2])])
        own = fresh
        steps = chan_steps(projected)
        gains = []
        for c in range(len(chunks)):
            blocks, got, bit = own[c][None], arrived[c][0], line // 2
            if len(arrived[c]) > 1:
                gains.append([blocks] + [arrived[c][direct_order.index(r)] for r in range(1, line)])
                continue
            after = JOIN_AFTER[iteration][min(c, 1)]
            while bit > 1:
                if after:
                    blocks = join(blocks, got, [steps[after]])
                else:
                    blocks = jnp.stack([blocks, got], axis=1).reshape((2 * blocks.shape[0],) + blocks.shape[1:])
                bit //= 2
                got = swap(blocks, "bl", line, bit)
            gains.append([blocks, got])
        if first:
            targets, duals = smooth(chunks, True, table, steps[-1], own, [], own_dims, [])
    consensus, dual = smooth(chunks, False, table, steps[-1], own, [duals], own_dims, [])
    return assemble(chunks, line, index, gains, dims), consensus, dual


def solution(mesh):
    in_specs = (
        P(None, None, "chan", "bl"),
        P(None, None, None, "chan", "bl"),
        P(None, None, None, "chan", None),
        P(),
        P(None, "bl"),
    )
    out_specs = (
        P(None, None, None, "chan", None),
        P(None, None, None, "chan", "bl"),
        P(None, None, None, "chan", "bl"),
    )
    return jax.shard_map(shards, mesh=mesh, in_specs=in_specs, out_specs=out_specs, check_vma=False)
```

```python
import functools
import math

import jax
import jax.numpy as jnp
import numpy as np
from jax import lax
from jax.experimental import pallas as pl
from jax.experimental.pallas import tpu as pltpu
from jax.sharding import PartitionSpec as P

POLY = 4
ITERS = 2
LANES = 128
SUBLANES = 8
JOIN_AFTER = ((0, 0), (1, 2))
ADD_AFTER = 2
ROWS_BY_COLS = (((1,), (0,)), ((), ()))
ROWS_BY_ROWS = (((1,), (1,)), ((), ()))
VMEM = pltpu.MemorySpace.VMEM
HBM = pltpu.MemorySpace.HBM
WHOLE = pl.BlockSpec(memory_space=VMEM)
OUTSIDE = pl.BlockSpec(memory_space=pl.ANY)
CHEAP = pl.CostEstimate(flops=2**20, bytes_accessed=2**10, transcendentals=0)


def run(kernel, token, in_specs, out_shape, operands, scratch=(), limit=4):
    count = len(token)
    return pl.pallas_call(
        lambda *refs: kernel(*refs[count:]),
        in_specs=[OUTSIDE] * count + list(in_specs),
        out_specs=[WHOLE] * len(out_shape),
        out_shape=list(out_shape),
        scratch_shapes=list(scratch),
        compiler_params=pltpu.CompilerParams(vmem_limit_bytes=limit * 2**20),
        cost_estimate=CHEAP,
    )(*token, *operands)


def bernstein_tables(total):
    position = (np.arange(total) + 0.5) / total
    basis = np.stack(
        [math.comb(POLY - 1, j) * position**j * (1.0 - position) ** (POLY - 1 - j) for j in range(POLY)], axis=1
    )
    factor = np.linalg.cholesky(basis.T @ basis)
    solved = np.linalg.solve(factor.T, np.linalg.solve(factor, basis.T)).T
    return basis.astype(np.float32), solved.astype(np.float32)


def split(values):
    upper = values.astype(jnp.bfloat16)
    return upper, (values - upper.astype(jnp.float32)).astype(jnp.bfloat16)


def chunks_of(times, chans):
    return [(t, t + 1, 0, chans) for t in range(times)]


def block_of(refs, r):
    return refs[r % 2][r // 2] if len(refs) == 2 else refs[r][0]


def normals_kernel(chunk, line, share, start, fill, sources, *refs):
    t0, t1, f0, f1 = chunk
    refs = list(refs)
    gain_refs = [refs.pop(0) for _ in range(sources)]
    vis_ref, coh_ref, pick_ref = [refs.pop(0) for _ in range(3)]
    outs = [refs.pop(0) for _ in range(2)]
    own_ref = refs.pop(0) if start else None
    dirs, links = coh_ref.shape[1], coh_ref.shape[4]
    rows = (t1 - t0) * (f1 - f0)
    copies = []
    if fill:
        offsets = block_offsets(line, share)
        moves = [(r * share, share, pl.multiple_of(offsets[r], LANES)) for r in range(line)]
        if share % LANES:
            moves = [(0, line * share, 0)]
        station_hbm, pick_ref = pick_ref, refs.pop(0)
        station_ref, sems = refs[-2:]
        pairs = [(station_hbm, station_ref)]
        for t in range(vis_ref.shape[1]):
            for to, size, at in moves:
                gain_from = gain_refs[0].at[:, :, t, :, pl.ds(at, size)]
                pairs.append((gain_from, refs[0].at[:, :, t, :, pl.ds(to, size)]))
            pairs += [(vis_ref.at[:, t], refs[1].at[:, t]), (coh_ref.at[:, :, t], refs[2].at[:, :, t])]
        each = len(moves) + 2
        gain_refs, vis_ref, coh_ref = [refs[0]], refs[1], refs[2]
        copies = [pltpu.make_async_copy(src, dst, sems.at[i]) for i, (src, dst) in enumerate(pairs)]
        for copy in copies:
            copy.start()
        copies[0].wait()
        for t in range(t0, t1):
            for copy in copies[1 + each * t : each * t + each - 1]:
                copy.wait()
        build_picks(line, share, offsets, station_ref, pick_ref)
    if start:
        blocks = [gain_refs[0][:, :, t0:t1, f0:f1, r * share : (r + 1) * share] for r in range(line)]
        own_ref[...] = blocks[0]
    else:
        blocks = [block_of(gain_refs, r) for r in range(line)]
    blocks = [block.reshape(2 * dirs * rows, share) for block in blocks]
    dot = functools.partial(lax.dot_general, preferred_element_type=jnp.float32)
    both = jnp.concatenate(split(jnp.concatenate(blocks, axis=1)), axis=0)
    wide = [dot(both, pick_ref[end], ROWS_BY_COLS) for end in range(2)]
    height = 2 * dirs * rows
    first, second = [values[:height] + values[height:] for values in wide]

    def row(values, part, k):
        begin = (part * dirs + k) * rows
        return values[begin : begin + rows]

    def coherency(part, k):
        low = f0 // 16 * 16
        high = min(-(-f1 // 16) * 16, coh_ref.shape[3])
        values = coh_ref[part, k, t0:t1, low:high].astype(jnp.float32)
        return values[:, f0 - low : f1 - low].reshape(rows, links)

    for t in range(t0, t1 if fill else t0):
        copies[each * t + each - 1].wait()
        copies[each * t + each].wait()
    rest_real = vis_ref[0, t0:t1, f0:f1].reshape(rows, links)
    rest_imag = vis_ref[1, t0:t1, f0:f1].reshape(rows, links)
    sides = []
    for k in range(dirs):
        coh_real, coh_imag = coherency(0, k), coherency(1, k)
        first_real, first_imag = row(first, 0, k), row(first, 1, k)
        second_real, second_imag = row(second, 0, k), row(second, 1, k)
        left_real = second_real * coh_real + second_imag * coh_imag
        left_imag = second_imag * coh_real - second_real * coh_imag
        right_real = first_real * coh_real - first_imag * coh_imag
        right_imag = first_real * coh_imag + first_imag * coh_real
        rest_real = rest_real - (first_real * left_real + first_imag * left_imag)
        rest_imag = rest_imag - (first_imag * left_real - first_real * left_imag)
        sides.append((left_real, left_imag, right_real, right_imag))
    terms = [[], []]
    terms[0] += [rest_real * a - rest_imag * b for a, b, _, _ in sides]
    terms[0] += [rest_real * b + rest_imag * a for a, b, _, _ in sides]
    terms[0] += [a * a + b * b for a, b, _, _ in sides]
    terms[1] += [rest_real * c + rest_imag * d for _, _, c, d in sides]
    terms[1] += [rest_real * d - rest_imag * c for _, _, c, d in sides]
    terms[1] += [c * c + d * d for _, _, c, d in sides]
    pieces = [split(jnp.concatenate(terms[end], axis=0)) for end in range(2)]
    wide = jnp.concatenate([pick_ref[0], pick_ref[1]], axis=1)
    total = None
    for part in range(2):
        value = dot(jnp.concatenate([pieces[0][part], pieces[1][part]], axis=1), wide, ROWS_BY_ROWS)
        total = value if total is None else total + value
    for r in range(line):
        piece = total[:, r * share : (r + 1) * share].reshape(3, dirs, t1 - t0, f1 - f0, share)
        outs[r % 2][r // 2] = piece
    for t in range(vis_ref.shape[1] if fill else 0):
        if not t0 <= t < t1:
            for copy in copies[1 + each * t : 1 + each * t + each]:
                copy.wait()


def block_offsets(line, share):
    place = lax.axis_index("bl")
    return [(place ^ r) * share for r in range(line)]


def build_picks(line, share, offsets, station_ref, pick_ref):
    links = station_ref.shape[1]
    one, zero = jnp.ones((), jnp.bfloat16), jnp.zeros((), jnp.bfloat16)
    ids = lax.broadcasted_iota(jnp.int32, (share, links), 0).astype(jnp.float32).astype(jnp.bfloat16)
    for end in range(2):
        for r in range(line):
            number = station_ref[end : end + 1, :] - offsets[r]
            number = jnp.where((number >= 0) & (number < share), number, -1)
            number = number.astype(jnp.float32).astype(jnp.bfloat16)
            pick_ref[end, r * share : (r + 1) * share] = jnp.where(ids == number, one, zero)


def picks_kernel(line, share, station_ref, pick_ref):
    build_picks(line, share, block_offsets(line, share), station_ref, pick_ref)


def make_picks(line, count, stations, token):
    shapes = [VMEM((2, count, stations.shape[1]), jnp.bfloat16)]
    kernel = functools.partial(picks_kernel, line, count // line)
    return run(kernel, token, [WHOLE], shapes, [stations], (), 8)[0]


def normals(chunk, line, start, fill, gains, visibilities, coherencies, picks, token):
    t0, t1, f0, f1 = chunk
    dirs, links = coherencies.shape[1], coherencies.shape[4]
    count = gains[0].shape[-1] if start else gains[0].shape[-1] * line
    share = count // line
    piece = (dirs, t1 - t0, f1 - f0, share)
    shapes = [jax.ShapeDtypeStruct((line // 2, 3) + piece, jnp.float32)] * 2
    scratch = []
    if start:
        shapes.append(jax.ShapeDtypeStruct((2,) + piece, jnp.float32))
    if fill:
        shapes.append(VMEM((2, count, links), jnp.bfloat16))
        times = visibilities.shape[1]
        scratch = [pltpu.VMEM((2, links), jnp.int32), pltpu.SemaphoreType.DMA((1 + (line + 2) * times,))]
        shapes += [VMEM(x.shape, x.dtype) for x in (gains[0], visibilities, coherencies)]
    spaces = [HBM if fill else VMEM] * (len(gains) + 3)
    sources = [*gains, visibilities, coherencies, picks]
    sources = [pltpu.with_memory_space_constraint(x, space) for x, space in zip(sources, spaces)]
    specs = [OUTSIDE if space is HBM else WHOLE for space in spaces]
    kernel = functools.partial(normals_kernel, chunk, line, share, start, fill, len(gains))
    return run(kernel, token, specs, shapes, sources, scratch, 32)


def add_kernel(keep_ref, got_ref, own_ref, send_ref):
    for i in range(own_ref.shape[0]):
        own_ref[i] = keep_ref[2 * i] + got_ref[2 * i]
        send_ref[i] = keep_ref[2 * i + 1] + got_ref[2 * i + 1]


def add_parts(keep, got, token):
    shape = jax.ShapeDtypeStruct((keep.shape[0] // 2,) + keep.shape[1:], keep.dtype)
    return run(add_kernel, token, [WHOLE] * 2, [shape] * 2, [keep, got])


def join_kernel(blocks_ref, got_ref, out_ref):
    for i in range(blocks_ref.shape[0]):
        out_ref[2 * i] = blocks_ref[i]
        out_ref[2 * i + 1] = got_ref[i]


def join(blocks, got, token):
    shape = jax.ShapeDtypeStruct((2 * blocks.shape[0],) + blocks.shape[1:], blocks.dtype)
    return run(join_kernel, token, [WHOLE] * 2, [shape], [blocks, got])[0]


def update_kernel(chunk, parts, first, penalty_ref, table_ref, before_ref, *refs):
    t0, t1, f0, f1 = chunk
    part_refs = refs[:parts]
    extra = refs[parts:-2]
    new_ref, sum_ref = refs[-2:]
    sum_ref[...] = before_ref[...]
    basis = table_ref[f0:f1]
    for k in range(new_ref.shape[1]):
        load = penalty_ref[k : k + 1]
        for t in range(t0, t1):
            weight = sum(ref[0, 2, k, t - t0] for ref in part_refs)
            divisor = weight + load
            for part in range(2):
                gain = extra[0][part, k, t - t0]
                target = gain if first else extra[1][part, k, t, f0:f1]
                total = sum(ref[0, part, k, t - t0] for ref in part_refs)
                new = (total + gain * weight + load * target) / divisor
                new_ref[part, k, t - t0] = new
                value = new if first else new + extra[2][part, k, t, f0:f1]
                for j in range(POLY):
                    row = jnp.sum(basis[:, j : j + 1] * value, axis=0, keepdims=True)
                    sum_ref[t, j, part, k : k + 1] += row


def update(chunk, first, penalty, table, before, parts, extra, token):
    shapes = [
        jax.ShapeDtypeStruct((2,) + parts[0].shape[2:], jnp.float32),
        jax.ShapeDtypeStruct(before.shape, jnp.float32),
    ]
    operands = [penalty, table, before, *parts, *extra]
    kernel = functools.partial(update_kernel, chunk, len(parts), first)
    return run(kernel, token, [WHOLE] * len(operands), shapes, operands)


def smooth_kernel(chunks, first, table_ref, sum_ref, *refs):
    one_ref, two_ref = refs[-2:]
    solved = table_ref[:, POLY:]
    for (t0, t1, f0, f1), gain_ref in zip(chunks, refs):
        for part in range(2):
            for k in range(one_ref.shape[1]):
                for t in range(t0, t1):
                    flat = sum(
                        solved[f0:f1, j : j + 1] * sum_ref[t, j, part, k : k + 1] for j in range(POLY)
                    )
                    value = gain_ref[part, k, t - t0]
                    at = (part, k, t, slice(f0, f1))
                    if first:
                        dual = value - flat
                        one_ref[at] = flat - dual
                    else:
                        dual = refs[len(chunks)][at] + value - flat
                        one_ref[at] = flat
                    two_ref[at] = dual


def smooth(chunks, first, table, sums, gains, extra, dims, token):
    operands = [table, sums, *gains, *extra]
    shapes = [jax.ShapeDtypeStruct(dims, jnp.float32)] * 2
    kernel = functools.partial(smooth_kernel, chunks, first)
    return run(kernel, token, [WHOLE] * len(operands), shapes, operands)


def assemble_kernel(chunks, sizes, line, share, *refs):
    out_ref = refs[-1]
    refs = list(refs)
    offsets = block_offsets(line, share)
    for size, (t0, t1, f0, f1) in zip(sizes, chunks):
        blocks = [refs.pop(0) for _ in range(size)]
        for r in range(line):
            offset = pl.multiple_of(offsets[r], LANES)
            out_ref[:, :, t0:t1, f0:f1, pl.ds(offset, share)] = block_of(blocks, r)


def assemble(chunks, line, place, gains, dims):
    share = dims[-1] // line
    if share % LANES:
        whole = jnp.zeros(dims, jnp.float32)
        for (t0, t1, f0, f1), blocks in zip(chunks, gains):
            stacked = jnp.stack([block_of(blocks, r) for r in range(line)])
            parts = [lax.dynamic_index_in_dim(stacked, place ^ r, 0, False) for r in range(line)]
            whole = whole.at[:, :, t0:t1, f0:f1].set(jnp.concatenate(parts, axis=-1))
        return whole
    flat = [block for blocks in gains for block in blocks]
    kernel = functools.partial(assemble_kernel, chunks, [len(blocks) for blocks in gains], line, share)
    shapes = [jax.ShapeDtypeStruct(dims, jnp.float32)]
    return run(kernel, [], [WHOLE] * len(flat), shapes, flat)[0]


def shards(visibilities, coherencies, start_gains, penalty, stations):
    dims = start_gains.shape
    _, dirs, times, chans, count = dims
    line = lax.axis_size("bl")
    index = lax.axis_index("bl")
    groups = lax.axis_size("chan")
    share = count // line
    tables = jnp.asarray(np.concatenate(bernstein_tables(chans * groups), axis=1))
    table = lax.dynamic_slice_in_dim(tables, lax.axis_index("chan") * chans, chans, 0)
    loads = jnp.broadcast_to(penalty[:, None], (dirs, share))

    def swap(values, axis, size, bit):
        return lax.ppermute(values, axis, [(i, i ^ bit) for i in range(size)])

    def chan_steps(values):
        steps = [values]
        bit = 1
        while bit < groups:
            steps.append(steps[-1] + swap(steps[-1], "chan", groups, bit))
            bit *= 2
        return steps

    ordered = start_gains
    if share % LANES:
        parts = [lax.dynamic_slice_in_dim(start_gains, (index ^ r) * share, share, 4) for r in range(line)]
        ordered = jnp.concatenate(parts, axis=4)
    own_dims = dims[:4] + (share,)
    chunks = chunks_of(times, chans)
    token = []
    gains = own = targets = duals = projected = None

    direct_order = list(range(1, line))
    zeros = jnp.zeros((times, POLY, 2, dirs, share), jnp.float32)
    for iteration in range(ITERS):
        first = iteration == 0
        parts, fresh = [], []
        if not first:
            picks = make_picks(line, count, stations, [own[0]])
            token = [picks]
        for c, chunk in enumerate(chunks):
            fill = first and c == 0
            source = [ordered] if first else gains[c]
            ends = stations if fill else picks
            out = normals(chunk, line, first, fill, source, visibilities, coherencies, ends, token)
            token = [out[0]]
            parts.append([out[0], swap(out[1], "bl", line, 1)])
            rest = list(out[2:])
            if first:
                fresh.append(rest.pop(0))
            if fill:
                picks, ordered, visibilities, coherencies = rest
        if first:
            own = fresh
        bit = 2
        while bit < line:
            for c in range(len(chunks)):
                waits = [steps[ADD_AFTER]] if ADD_AFTER and c and not first else []
                keep, send = add_parts(*parts[c], token + waits)
                parts[c] = [keep, swap(send, "bl", line, bit)]
                token = [keep]
            bit *= 2
        fresh, arrived = [], []
        projected = zeros
        for c, chunk in enumerate(chunks):
            extra = [own[c]] if first else [own[c], targets, duals]
            new, projected = update(chunk, first, loads, table, projected, parts[c], extra, token)
            token = [new]
            fresh.append(new)
            direct = c == len(chunks) - 1
            arrived.append([swap(new[None], "bl", line, r) for r in (direct_order if direct else [line // 2])])
        own = fresh
        steps = chan_steps(projected)
        gains = []
        for c in range(len(chunks)):
            blocks, got, bit = own[c][None], arrived[c][0], line // 2
            if len(arrived[c]) > 1:
                gains.append([blocks] + [arrived[c][direct_order.index(r)] for r in range(1, line)])
                continue
            after = JOIN_AFTER[iteration][min(c, 1)]
            while bit > 1:
                if after:
                    blocks = join(blocks, got, [steps[after]])
                else:
                    blocks = jnp.stack([blocks, got], axis=1).reshape((2 * blocks.shape[0],) + blocks.shape[1:])
                bit //= 2
                got = swap(blocks, "bl", line, bit)
            gains.append([blocks, got])
        if first:
            targets, duals = smooth(chunks, True, table, steps[-1], own, [], own_dims, [])
    consensus, dual = smooth(chunks, False, table, steps[-1], own, [duals], own_dims, [])
    return assemble(chunks, line, index, gains, dims), consensus, dual


def solution(mesh):
    in_specs = (
        P(None, None, "chan", "bl"),
        P(None, None, None, "chan", "bl"),
        P(None, None, None, "chan", None),
        P(),
        P(None, "bl"),
    )
    out_specs = (
        P(None, None, None, "chan", None),
        P(None, None, None, "chan", "bl"),
        P(None, None, None, "chan", "bl"),
    )
    return jax.shard_map(shards, mesh=mesh, in_specs=in_specs, out_specs=out_specs, check_vma=False)
```
